256 devices in a mesh: dp: 8 (over x, core), ctx: 32 (over y, z).
Axes of the slice: x: 4, y: 4, z: 8, core: 2. Of those that a mesh axis runs over, the one named last changes fastest.
Arguments:
- queries: bfloat16 [8, 8192, 512], P('dp', 'ctx'), may hold values from -6 to 6
- keys: bfloat16 [8, 8192, 512], P('dp', 'ctx'), may hold values from -6 to 6
- values: bfloat16 [8, 8192, 512], P('dp', 'ctx'), may hold values from -6 to 6
- out_weight: bfloat16 [512, 2048], replicated, may hold values from -0.25 to 0.25
- cotangent: bfloat16 [8, 8192, 2048], P('dp', 'ctx'), may hold values from -6 to 6
- prefix: int32 [8], P('dp'), may hold values from 0 to 64
Outputs:
- mixed: bfloat16 [8, 8192, 2048], P('dp', 'ctx')
- query_grad: float32 [8, 8192, 512], P('dp', 'ctx')
- key_grad: float32 [8, 8192, 512], P('dp', 'ctx')
- value_grad: float32 [8, 8192, 512], P('dp', 'ctx')
- weight_grad: float32 [512, 2048], P(('dp', 'ctx'))
The draws below stay inside these ranges and needn't reach their ends.
All inputs are finite; a program needn't handle non-finite values.
Results may differ from the reference program's by a relative error of at most 0.029.
Values may be sent and summed in bfloat16 or wider, within the bound.
A program may use at most 128 MiB of HBM per device.

```python
import jax
import jax.numpy as jnp
from jax import lax

HEADS = 4
HEAD_DIM = 128
D = 2048
BLOCK = 128
HD = 512
TOK_DEV = 256
SEQS = 8
LEN = 8192
NBLOCKS = 64
LEVELS = 2
N_CTX = 32


def draw_queries(key, part):
    key = jax.random.fold_in(key, 5)
    full_shape = (SEQS, LEN, HEADS * HEAD_DIM)
    return jnp.clip(jax.random.normal(key, full_shape, jnp.float32), -6.0, 6.0).astype(jnp.bfloat16)


def draw_keys(key, part):
    key = jax.random.fold_in(key, 9)
    full_shape = (SEQS, LEN, HEADS * HEAD_DIM)
    return jnp.clip(jax.random.normal(key, full_shape, jnp.float32), -6.0, 6.0).astype(jnp.bfloat16)


def with_ends(values, key, least, top_value):
    longest = values.shape.index(max(values.shape))
    spots = []
    for shift in (0, 1):
        where = [jax.random.randint(jax.random.fold_in(key, axis), (), 0, length) for axis, length in enumerate(values.shape)]
        where[longest] = (where[longest] + shift) % values.shape[longest]
        spots.append(tuple(where))
    return values.at[spots[0]].set(least).at[spots[1]].set(top_value)


def spiked(values, key, source, target, parts, factor):
    def block_of(axis_at):
        return (jnp.arange(values.shape[axis_at]) // (values.shape[axis_at] // parts)).reshape((-1,) + (1,) * (values.ndim - 1 - axis_at))

    first = jax.random.permutation(key, parts)[block_of(target)]
    other_side = (block_of(target) + parts // 2) % parts
    return jnp.where((block_of(source) == first) | (block_of(source) == other_side), factor * values, values)


def steps_of(rng, dims, cuts, least, top_value):
    loudness = 1.0
    for dim, shards_of in cuts:
        heights = jax.random.uniform(jax.random.fold_in(jax.random.fold_in(rng, 6), dim), (shards_of,), jnp.float32, least / len(cuts), top_value / len(cuts))
        loudness = loudness * jnp.repeat(jnp.exp(heights), dims[dim] // shards_of).reshape((-1,) + (1,) * (len(dims) - 1 - dim))
    return loudness


def bell_draw(rng, extent, scale, bound, cuts=(), kind=jnp.bfloat16):
    loudness = steps_of(rng, extent, cuts, -0.22, 0.18) if cuts else 1.0
    array = jax.random.normal(rng, extent, jnp.float32) * scale * loudness
    return jnp.minimum(jnp.maximum(array, -bound), bound).astype(kind)


def bell_draw_with(stream_key, dims, spread, most, split, heavy, kind=jnp.bfloat16):
    values = spread * jax.random.normal(stream_key, dims, jnp.float32)
    if split:
        values = values * steps_of(stream_key, dims, split, -0.22, 0.18)
    return jnp.clip(spiked(values, jax.random.fold_in(stream_key, 3), *heavy), -most, most).astype(kind)


def setup_inputs(seed: int = 0) -> dict:
    key_of = jax.random.split(jax.random.key(seed), 7)
    queries = draw_queries(jax.random.fold_in(key_of[6], 71), 0)
    keys = draw_keys(jax.random.fold_in(key_of[6], 71), 0)
    values = bell_draw(key_of[2], (SEQS, LEN, HD), 1.0, 6.0, ((0, 8), (1, 32)))
    out_weight = bell_draw(key_of[3], (HD, D), HD ** -0.5, 0.25)
    cotangent = bell_draw_with(key_of[4], (SEQS, LEN, D), 1.0, 6.0, ((0, 8), (1, 32)), (1, 2, 32, 2.75))
    prefix = with_ends(jax.random.randint(key_of[5], (SEQS,), 0, NBLOCKS + 1), jax.random.fold_in(key_of[5], 1), 0, NBLOCKS).astype(jnp.int32)
    return {"queries": queries, "keys": keys, "values": values, "out_weight": out_weight, "cotangent": cotangent, "prefix": prefix}


def level_masks(device_pos, prefix_len):
    first_row = device_pos * TOK_DEV
    row_pos = first_row + jnp.arange(TOK_DEV, dtype=jnp.int32)
    prefix_end = prefix_len * BLOCK
    col_pos = first_row - BLOCK + jnp.arange(TOK_DEV + 2 * BLOCK, dtype=jnp.int32)
    nearby = jnp.abs(col_pos[None, :] // BLOCK - row_pos[:, None] // BLOCK) <= 1
    inside = (col_pos >= 0) & (col_pos < LEN)
    allowed = (col_pos[None, :] < prefix_end) | (col_pos[None, :] <= row_pos[:, None])
    mask_list = [nearby & inside[None, :] & allowed]
    weight_list = [jnp.ones((TOK_DEV + 2 * BLOCK,), jnp.float32)]
    for level in range(1, LEVELS + 1):
        level_ratio = 2 ** level
        parent_idx = device_pos // level_ratio
        own_block = device_pos // (level_ratio // 2)
        entries = (parent_idx - 1) * 2 * BLOCK + jnp.arange(6 * BLOCK, dtype=jnp.int32)
        blocks = entries // BLOCK
        listed = (blocks >= 0) & (blocks < LEN // (BLOCK * level_ratio)) & (jnp.abs(blocks - own_block) >= 2)
        usable = listed & ((blocks < own_block) | ((entries + 1) * level_ratio <= prefix_end))
        mask_list.append(jnp.broadcast_to(usable[None, :], (TOK_DEV, 6 * BLOCK)))
        weight_list.append(jnp.full((6 * BLOCK,), float(level_ratio), jnp.float32))
    return jnp.concatenate(mask_list, axis=1), jnp.concatenate(weight_list)


def one_sequence(seq_args, out_weight):
    q_seq, k_seq, v_seq, grad_out, prefix_len = seq_args
    feat_width = q_seq.shape[1]
    model_width = out_weight.shape[1]
    score_scale = HEAD_DIM ** -0.5
    highest = lax.Precision.HIGHEST
    key_value = jnp.stack([k_seq, v_seq])
    fine_pad = jnp.pad(key_value, ((0, 0), (BLOCK, BLOCK), (0, 0)))
    coarse_pad = []
    for level in range(1, LEVELS + 1):
        level_ratio = 2 ** level
        coarse = jnp.mean(key_value.reshape(2, LEN // level_ratio, level_ratio, feat_width), axis=2, dtype=jnp.float32).astype(jnp.bfloat16)
        coarse_pad.append(jnp.pad(coarse, ((0, 0), (2 * BLOCK, 2 * BLOCK), (0, 0))))
    grad_attended = jnp.dot(grad_out, out_weight.T, preferred_element_type=jnp.float32).astype(jnp.bfloat16)
    fine_span = TOK_DEV + 2 * BLOCK

    def scan_step(accum, device_pos):
        fine_acc, coarse_acc, weight_acc = accum
        first_row = device_pos * TOK_DEV
        query_rows = lax.dynamic_slice_in_dim(q_seq, first_row, TOK_DEV, 0)
        out_rows = lax.dynamic_slice_in_dim(grad_out, first_row, TOK_DEV, 0)
        back_rows = lax.dynamic_slice_in_dim(grad_attended, first_row, TOK_DEV, 0)
        pieces = [lax.dynamic_slice_in_dim(fine_pad, first_row, fine_span, 1)]
        for level in range(1, LEVELS + 1):
            parent_idx = device_pos // (2 ** level)
            pieces.append(lax.dynamic_slice_in_dim(coarse_pad[level - 1], parent_idx * 2 * BLOCK, 6 * BLOCK, 1))
        window = jnp.concatenate(pieces, axis=1)
        key_count = window.shape[1]
        key_heads = window[0].astype(jnp.float32).reshape(key_count, HEADS, HEAD_DIM)
        value_heads = window[1].astype(jnp.float32).reshape(key_count, HEADS, HEAD_DIM)
        query_heads = query_rows.astype(jnp.float32).reshape(TOK_DEV, HEADS, HEAD_DIM)
        live_mask, weights = level_masks(device_pos, prefix_len)
        scores = jnp.einsum("the,khe->htk", query_heads, key_heads, precision=highest) * score_scale
        row_peak = jnp.max(jnp.where(live_mask[None], scores, -jnp.inf), axis=2, keepdims=True)
        exp_scores = jnp.where(live_mask[None], jnp.exp(scores - row_peak), 0.0)
        norm_total = jnp.sum(exp_scores * weights, axis=2, keepdims=True)
        weighted = (exp_scores * weights).astype(jnp.bfloat16)
        summed = jnp.einsum("htk,khe->the", weighted.astype(jnp.float32), value_heads, precision=highest)
        attended = (summed / jnp.transpose(norm_total, (1, 0, 2))).astype(jnp.bfloat16).reshape(TOK_DEV, feat_width)
        mixed_rows = jnp.dot(attended, out_weight, preferred_element_type=jnp.float32).astype(jnp.bfloat16)
        weight_acc = weight_acc + jnp.dot(attended.T, out_rows, preferred_element_type=jnp.float32)
        back_heads = back_rows.astype(jnp.float32).reshape(TOK_DEV, HEADS, HEAD_DIM)
        probability = exp_scores * weights / norm_total
        prob_half = probability.astype(jnp.bfloat16)
        row_delta = jnp.sum(back_heads * attended.astype(jnp.float32).reshape(TOK_DEV, HEADS, HEAD_DIM), axis=2)
        row_delta = jnp.transpose(row_delta)[:, :, None]
        prob_grad = jnp.einsum("the,khe->htk", back_heads, value_heads, precision=highest)
        score_grad = (probability * (prob_grad - row_delta)).astype(jnp.bfloat16).astype(jnp.float32)
        query_grad = jnp.einsum("htk,khe->the", score_grad, key_heads, precision=highest) * score_scale
        key_part = jnp.einsum("htk,the->khe", score_grad, query_heads, precision=highest) * score_scale
        value_part = jnp.einsum("htk,the->khe", prob_half.astype(jnp.float32), back_heads, precision=highest)
        window_grad = jnp.stack([key_part.reshape(key_count, feat_width), value_part.reshape(key_count, feat_width)])
        old_fine = lax.dynamic_slice_in_dim(fine_acc, first_row, fine_span, 1)
        fine_acc = lax.dynamic_update_slice_in_dim(fine_acc, old_fine + window_grad[:, :fine_span], first_row, 1)
        new_coarse = []
        for level in range(1, LEVELS + 1):
            parent_idx = device_pos // (2 ** level)
            begin_row = parent_idx * 2 * BLOCK
            offset = fine_span + (level - 1) * 6 * BLOCK
            old_part = lax.dynamic_slice_in_dim(coarse_acc[level - 1], begin_row, 6 * BLOCK, 1)
            new_part = old_part + window_grad[:, offset:offset + 6 * BLOCK]
            new_coarse.append(lax.dynamic_update_slice_in_dim(coarse_acc[level - 1], new_part, begin_row, 1))
        return (fine_acc, tuple(new_coarse), weight_acc), (mixed_rows, query_grad.reshape(TOK_DEV, feat_width))

    fine_zero = jnp.zeros((2, LEN + 2 * BLOCK, feat_width), jnp.float32)
    coarse_zero = tuple(jnp.zeros((2, LEN // (2 ** level) + 4 * BLOCK, feat_width), jnp.float32) for level in range(1, LEVELS + 1))
    weight_zero = jnp.zeros((feat_width, model_width), jnp.float32)
    accum, stacked = lax.scan(scan_step, (fine_zero, coarse_zero, weight_zero), jnp.arange(N_CTX, dtype=jnp.int32))
    fine_acc, coarse_acc, weight_acc = accum
    grad_total = fine_acc[:, BLOCK:BLOCK + LEN]
    for level in range(1, LEVELS + 1):
        level_ratio = 2 ** level
        owned = coarse_acc[level - 1][:, 2 * BLOCK:2 * BLOCK + LEN // level_ratio]
        grad_total = grad_total + jnp.repeat(owned, level_ratio, axis=1) / level_ratio
    mixed_seq = stacked[0].reshape(LEN, model_width)
    query_seq = stacked[1].reshape(LEN, feat_width)
    return mixed_seq, query_seq, grad_total[0], grad_total[1], weight_acc


def reference(queries, keys, values, out_weight, cotangent, prefix):
    results = lax.map(lambda seq_args: one_sequence(seq_args, out_weight), (queries, keys, values, cotangent, prefix))
    mixed, query_grad, key_grad, value_grad, weight_terms = results
    return mixed, query_grad, key_grad, value_grad, jnp.sum(weight_terms, axis=0)
```

```python
import jax
import jax.numpy as jnp
from jax import lax
from jax.experimental import pallas as pl
from jax.experimental.pallas import tpu as pltpu
from jax.sharding import PartitionSpec as P

HEADS = 4
HEAD_DIM = 128
BLOCK = 128
D = 2048
HD = 512
TOK = 256
LEN = 8192
CTX = 32
KEYS = 1280
SCALE = HEAD_DIM**-0.5
LOG2E = 1.4426950408889634
DEAD = -1e30
MESH = pl.DeviceIdType.MESH
F32 = jnp.float32
BF16 = jnp.bfloat16

PREV, OWN, NEXT, NEAR1, FAR1, THIRD1, NEAR2, FAR2, COPY2 = 0, 1, 3, 4, 5, 6, 7, 8, 9

(
    R_PREV,
    R_NEXT,
    R_NEAR1,
    R_FAR1,
    R_THIRD1,
    R_PAIR,
    R_NEAR2,
    R_FAR2,
    R_COPY2,
    B_PREV,
    B_NEXT,
    B_NEAR1,
    B_FAR1,
    B_THIRD1,
    B_COPY2,
    B_FAR2,
    B_NEAR2,
    B_PAIR,
    B_PIECE,
    W_CORE,
) = range(20)
KINDS = 20
G_PREV, G_NEXT, G_NEAR1, G_FAR1, G_THIRD1, G_COPY2, G_FAR2, G_NEAR2, G_PAIR, G_PIECE = range(10)


def dot(a, b, ca, cb):
    return lax.dot_general(a, b, (((ca,), (cb,)), ((), ())), preferred_element_type=F32)


def slot(index, count=1):
    return pl.ds(index * BLOCK, count * BLOCK)


def kernel(
    prefix_ref,
    q_ref,
    k_ref,
    v_ref,
    w_hbm,
    cot_hbm,
    mixed_hbm,
    dq_ref,
    dk_ref,
    dv_ref,
    dw_ref,
    w_ref,
    cot_ref,
    mixed_ref,
    win,
    co1,
    co2,
    pair2,
    bias,
    go_t,
    att_t,
    keep,
    gsend,
    grecv,
    rs_core_send,
    rs_core_recv,
    rs_x_send,
    rs_x_recv,
    rs_own,
    rs_y_send,
    rs_y_recv,
    rs_z_send,
    rs_z_recv,
    load_sem,
    send_sem,
    recv_sem,
    rs_recv_sem,
):
    dp = lax.axis_index("dp")
    me = lax.axis_index("ctx")
    x, core = lax.div(dp, 2), lax.rem(dp, 2)
    y, z = lax.div(me, 8), lax.rem(me, 8)
    r = lax.rem(me, 4)
    parity = lax.rem(me, 2)
    pi = 1 - 2 * parity
    tau = 1 - 2 * lax.div(r, 2)
    outer = (r == 0) | (r == 3)
    inner = (r == 1) | (r == 2)

    def ctx(offset):
        return (dp, lax.rem(me + offset + 2 * CTX, CTX))

    def row_peer(step):
        return (dp, y * 8 + lax.rem(z + step, 8))

    def column_peer(step):
        return (dp, lax.rem(y + step, 4) * 8 + z)

    sibling = (dp + 1 - 2 * core, me)

    load_w = pltpu.make_async_copy(w_hbm, w_ref, load_sem.at[0])
    load_cot = pltpu.make_async_copy(cot_hbm, cot_ref, load_sem.at[1])
    load_w.start()
    load_cot.start()

    barrier = pltpu.get_barrier_semaphore()
    partners = [ctx(o) for o in (1, -1, 2, -2, 7, -7, 8, -8, 16)]
    partners += [row_peer(s) for s in range(1, 8)]
    partners += [(lax.rem(x + s, 4) * 2 + core, me) for s in range(1, 4)]
    partners += [sibling]
    for partner in partners:
        pl.semaphore_signal(barrier, inc=1, device_id=partner, device_id_type=MESH)

    half = pl.multiple_of(parity * 64, 64)
    other_half = pl.multiple_of(64 - parity * 64, 64)
    entry = lax.broadcasted_iota(jnp.int32, (192, TOK), 0)
    token = lax.broadcasted_iota(jnp.int32, (192, TOK), 1)
    mean1 = (entry < 128) & (lax.shift_right_logical(token, 1) == entry)
    mean2 = (entry >= 128) & (lax.shift_right_logical(token, 2) == entry - 128)
    means = jnp.where(mean1, 0.5, jnp.where(mean2, 0.25, 0.0)).astype(BF16)
    for kv, source in enumerate((k_ref, v_ref)):
        coarse = dot(means, source[...], 1, 0).astype(BF16)
        for h in range(HEADS):
            cols = slice(h * HEAD_DIM, (h + 1) * HEAD_DIM)
            win[h, kv, OWN * BLOCK : (OWN + 2) * BLOCK, :] = source[:, cols]
            co1[h, kv] = coarse[:128, cols]
            co2[h, kv] = coarse[128:, cols]
            pair2[h, kv, pl.ds(half, 64), :] = coarse[128:, cols]

    pl.semaphore_wait(barrier, len(partners))

    started = []

    def send(sems, kind, src, dst, device, when=None):
        send_sems, recv_sems = sems
        copy = pltpu.make_async_remote_copy(
            src_ref=src,
            dst_ref=dst,
            send_sem=send_sems.at[len(started)],
            recv_sem=recv_sems.at[kind],
            device_id=device,
            device_id_type=MESH,
        )
        if when is None:
            copy.start()
        else:
            pl.when(when)(copy.start)
        started.append((when, copy))

    def arrive(sems, kind, dst, device):
        pltpu.make_async_remote_copy(
            src_ref=dst,
            dst_ref=dst,
            send_sem=sems[0].at[0],
            recv_sem=sems[1].at[kind],
            device_id=device,
            device_id_type=MESH,
        ).wait_recv()

    def sems(h):
        return send_sem, recv_sem.at[h]

    def window(h, index):
        return win.at[h, :, slot(index), :]

    def returned(h, index):
        return grecv.at[h, index]

    def first_sends(h):
        piece = pair2.at[h, :, pl.ds(half, 64), :]
        send(sems(h), R_PAIR, piece, piece, ctx(-tau), inner)
        send(sems(h), R_NEAR1, co1.at[h], window(h, NEAR1), ctx(2 * pi))
        send(sems(h), R_FAR1, co1.at[h], window(h, FAR1), ctx(-2 * pi))
        send(sems(h), R_NEXT, window(h, OWN), window(h, NEXT), ctx(-1))
        send(sems(h), R_PREV, window(h, OWN + 1), window(h, PREV), ctx(1))

    def relay_pair(h):
        @pl.when(outer)
        def _():
            arrive(sems(h), R_PAIR, pair2.at[h, :, pl.ds(other_half, 64), :], ctx(tau))

        send(sems(h), R_NEAR2, pair2.at[h], window(h, NEAR2), ctx(7 * tau), outer)

    def relay_near(h):
        arrive(sems(h), R_NEAR2, window(h, NEAR2), ctx(tau))
        send(sems(h), R_NEAR2, window(h, NEAR2), window(h, NEAR2), ctx(tau), outer)
        send(sems(h), R_FAR2, window(h, NEAR2), window(h, FAR2), ctx(tau), inner)
        arrive(sems(h), R_NEAR1, window(h, NEAR1), ctx(2 * pi))
        send(sems(h), R_THIRD1, window(h, NEAR1), window(h, THIRD1), ctx(pi))

    def relay_far(h):
        arrive(sems(h), R_FAR2, window(h, FAR2), ctx(tau))
        send(sems(h), R_FAR2, window(h, FAR2), window(h, FAR2), ctx(-tau), inner)
        send(sems(h), R_COPY2, window(h, FAR2), window(h, COPY2), ctx(-8 * tau))

    def last_arrivals(h):
        arrive(sems(h), R_NEXT, window(h, NEXT), ctx(1))
        arrive(sems(h), R_PREV, window(h, PREV), ctx(-1))
        arrive(sems(h), R_FAR1, window(h, FAR1), ctx(2 * pi))
        arrive(sems(h), R_THIRD1, window(h, THIRD1), ctx(pi))
        arrive(sems(h), R_COPY2, window(h, COPY2), ctx(8 * tau))

    def masks():
        prefix_end = prefix_ref[0] * BLOCK
        first_row = me * TOK
        key = lax.broadcasted_iota(jnp.int32, (4 * BLOCK, TOK), 0)
        query = lax.broadcasted_iota(jnp.int32, (4 * BLOCK, TOK), 1)
        apart = lax.shift_right_logical(key, 7) - lax.shift_right_logical(query, 7)
        column = first_row - BLOCK + key
        live = (apart >= 0) & (apart <= 2) & (column >= 0) & (column < LEN)
        live = live & ((column < prefix_end) | (column <= first_row + query))
        bias[: 4 * BLOCK, :] = jnp.where(live, 0.0, DEAD)
        quad = lax.div(me, 4)
        near2 = jnp.where(tau == 1, 2 * quad + 3, 2 * quad - 2)
        far2 = jnp.where(tau == 1, 2 * quad - 2, 2 * quad + 3)
        copy2 = jnp.where(tau == 1, 2 * quad + 2, 2 * quad - 1)
        level1 = [(NEAR1, me - 2 * pi), (FAR1, me + 2 * pi), (THIRD1, me + 3 * pi)]
        level2 = [(NEAR2, near2), (FAR2, far2), (COPY2, copy2)]
        place = lax.broadcasted_iota(jnp.int32, (BLOCK, TOK), 0)
        for level, entries in ((1, level1), (2, level2)):
            blocks = LEN // (BLOCK << level)
            own = lax.div(me, level)
            for index, block in entries:
                end = (block * BLOCK + place + 1) * (1 << level)
                inside = (block >= 0) & (block < blocks)
                before = jnp.where(inside & (block < own), LEN, 0)
                until = jnp.where(inside, prefix_end, 0)
                usable = (place < before) | ((end <= until) & (end > 0))
                bias[slot(index), :] = jnp.where(usable, float(level), DEAD)

    def attend(h):
        cols = slice(h * HEAD_DIM, (h + 1) * HEAD_DIM)
        key = win[h, 0]
        value = win[h, 1]
        query = q_ref[:, cols]
        scores = dot(key, query, 1, 1) * (SCALE * LOG2E) + bias[...]
        peak = jnp.max(scores, axis=0, keepdims=True)
        weighted = jnp.exp2(scores - peak)
        inverse = 1.0 / jnp.sum(weighted, axis=0, keepdims=True)
        weighted_half = weighted.astype(BF16)
        attended = (dot(value, weighted_half, 0, 0) * inverse).astype(BF16)
        att_t[cols, :] = attended
        back = go_t[cols, :].astype(F32)
        delta = jnp.sum(back * attended.astype(F32), axis=0, keepdims=True) * inverse
        back = (back * inverse).astype(BF16)
        score_grad = (weighted * (dot(value, back, 1, 0) - delta)).astype(BF16)
        dq_ref[:, cols] = jnp.transpose(dot(key, score_grad, 0, 0) * SCALE)
        for kv, grad in enumerate(
            (dot(score_grad, query, 1, 0) * SCALE, dot(weighted_half, back, 1, 1))
        ):
            own = dk_ref if kv == 0 else dv_ref
            own[:, cols] = grad[OWN * BLOCK : (OWN + 2) * BLOCK]
            gsend[h, kv, slot(0), :] = grad[:BLOCK].astype(BF16)
            gsend[h, kv, slot(1), :] = grad[NEXT * BLOCK : (NEXT + 1) * BLOCK].astype(BF16)
            gsend[h, kv, slot(2), :] = grad[FAR1 * BLOCK : (FAR1 + 1) * BLOCK].astype(BF16)
            gsend[h, kv, slot(3), :] = grad[THIRD1 * BLOCK : (THIRD1 + 1) * BLOCK].astype(BF16)
            gsend[h, kv, slot(4), :] = grad[COPY2 * BLOCK :].astype(BF16)
            keep[h, kv, slot(0), :] = grad[NEAR1 * BLOCK : (NEAR1 + 1) * BLOCK]
            keep[h, kv, slot(1), :] = grad[FAR2 * BLOCK : (FAR2 + 1) * BLOCK]
            keep[h, kv, slot(2), :] = grad[NEAR2 * BLOCK : (NEAR2 + 1) * BLOCK]

    def outgoing(h, index):
        return gsend.at[h, :, slot(index), :]

    def back_first(h):
        send(sems(h), B_COPY2, outgoing(h, 4), returned(h, G_COPY2), ctx(8 * tau))
        send(sems(h), B_THIRD1, outgoing(h, 3), returned(h, G_THIRD1), ctx(pi))
        send(sems(h), B_FAR1, outgoing(h, 2), returned(h, G_FAR1), ctx(2 * pi))
        send(sems(h), B_NEXT, outgoing(h, 0), returned(h, G_NEXT), ctx(-1))
        send(sems(h), B_PREV, outgoing(h, 1), returned(h, G_PREV), ctx(1))

    def back_far(h):
        arrive(sems(h), B_COPY2, returned(h, G_COPY2), ctx(-8 * tau))

        @pl.when(inner)
        def _():
            arrive(sems(h), B_FAR2, returned(h, G_FAR2), ctx(-tau))

        theirs = grecv[h, G_COPY2].astype(F32)
        more = jnp.where(inner, grecv[h, G_FAR2].astype(F32), 0.0)
        gsend[h, :, slot(6), :] = (keep[h, :, slot(1), :] + theirs + more).astype(BF16)
        send(sems(h), B_FAR2, outgoing(h, 6), returned(h, G_FAR2), ctx(tau), outer)
        send(sems(h), B_NEAR2, outgoing(h, 6), returned(h, G_NEAR2), ctx(tau), inner)
        arrive(sems(h), B_THIRD1, returned(h, G_THIRD1), ctx(pi))
        theirs = grecv[h, G_THIRD1].astype(F32)
        gsend[h, :, slot(5), :] = (keep[h, :, slot(0), :] + theirs).astype(BF16)
        send(sems(h), B_NEAR1, outgoing(h, 5), returned(h, G_NEAR1), ctx(-2 * pi))

    def back_near(h):
        arrive(sems(h), B_NEAR2, returned(h, G_NEAR2), ctx(tau))
        theirs = grecv[h, G_NEAR2].astype(F32)
        gsend[h, :, slot(7), :] = (keep[h, :, slot(2), :] + theirs).astype(BF16)
        send(sems(h), B_NEAR2, outgoing(h, 7), returned(h, G_NEAR2), ctx(-tau), inner)
        send(sems(h), B_PAIR, outgoing(h, 7), returned(h, G_PAIR), ctx(7 * tau), outer)

    def back_pair(h):
        @pl.when(outer)
        def _():
            arrive(sems(h), B_PAIR, returned(h, G_PAIR), ctx(7 * tau))

        theirs = grecv.at[h, G_PAIR, :, pl.ds(other_half, 64), :]
        mine = grecv.at[h, G_PIECE, :, pl.ds(0, 64), :]
        send(sems(h), B_PIECE, theirs, mine, ctx(tau), outer)

    def finish(h):
        cols = slice(h * HEAD_DIM, (h + 1) * HEAD_DIM)
        arrive(sems(h), B_NEXT, returned(h, G_NEXT), ctx(1))
        arrive(sems(h), B_PREV, returned(h, G_PREV), ctx(-1))
        arrive(sems(h), B_FAR1, returned(h, G_FAR1), ctx(-2 * pi))
        arrive(sems(h), B_NEAR1, returned(h, G_NEAR1), ctx(2 * pi))

        @pl.when(inner)
        def _():
            arrive(sems(h), B_PIECE, grecv.at[h, G_PIECE, :, pl.ds(0, 64), :], ctx(-tau))

        for kv, own in enumerate((dk_ref, dv_ref)):
            level1 = grecv[h, G_FAR1, kv].astype(F32) + grecv[h, G_NEAR1, kv].astype(F32)
            pair = grecv[h, G_PAIR, kv, pl.ds(half, 64), :]
            level2 = jnp.where(outer, pair, grecv[h, G_PIECE, kv, :64, :])
            entries = jnp.concatenate([level1.astype(BF16), level2], axis=0)
            spread = dot(means, entries, 0, 0)
            own[:BLOCK, cols] += spread[:BLOCK] + grecv[h, G_PREV, kv].astype(F32)
            own[BLOCK:, cols] += spread[BLOCK:] + grecv[h, G_NEXT, kv].astype(F32)

    def weight_part(h, which):
        rows = pl.ds(pl.multiple_of(h * HEAD_DIM + which * 64, 64), 64)
        return dot(att_t[rows, :], cot_ref[...], 1, 0)

    def weight_core(h):
        rs_core_send[h] = weight_part(h, 1 - core).astype(BF16)
        send(sems(h), W_CORE, rs_core_send.at[h], rs_core_recv.at[h], sibling)

    rs_sems = (send_sem, rs_recv_sem)

    def weight_x(h):
        arrive(sems(h), W_CORE, rs_core_recv.at[h], sibling)
        total = weight_part(h, core) + rs_core_recv[h].astype(F32)
        rs_x_send[h] = total.astype(BF16)

        @pl.when(x == h)
        def _():
            rs_own[...] = total

        step = lax.rem(x - h + 4, 4)
        place = jnp.maximum(step - 1, 0)
        send(rs_sems, place, rs_x_send.at[h], rs_x_recv.at[place], (h * 2 + core, me), x != h)

    def weight_y():
        for step in range(1, 4):
            device = (lax.rem(x + step, 4) * 2 + core, me)
            arrive(rs_sems, step - 1, rs_x_recv.at[step - 1], device)
        total = rs_own[...]
        for step in range(1, 4):
            total = total + rs_x_recv[step - 1].astype(F32)
        rs_own[...] = total
        rs_y_send[...] = total.astype(BF16)
        for step in range(1, 4):
            rows = pl.ds(pl.multiple_of(lax.rem(y + step, 4) * 16, 16), 16)
            send(rs_sems, 2 + step, rs_y_send.at[rows], rs_y_recv.at[step - 1], column_peer(step))

    def weight_z():
        for step in range(1, 4):
            arrive(rs_sems, 2 + step, rs_y_recv.at[step - 1], column_peer(step))
        total = rs_own[pl.ds(pl.multiple_of(y * 16, 16), 16), :]
        for step in range(1, 4):
            total = total + rs_y_recv[step - 1].astype(F32)
        for part in range(8):
            rs_z_send[part] = total[2 * part : 2 * part + 2]
        for step in range(1, 8):
            part = rs_z_send.at[lax.rem(z + step, 8)]
            send(rs_sems, 5 + step, part, rs_z_recv.at[step - 1], row_peer(step))

    def weight_end():
        for step in range(1, 8):
            arrive(rs_sems, 5 + step, rs_z_recv.at[step - 1], row_peer(step))
        total = rs_z_send[z]
        for step in range(1, 8):
            total = total + rs_z_recv[step - 1]
        dw_ref[...] = total

    for h in range(HEADS):
        first_sends(h)
    masks()
    load_w.wait()
    load_cot.wait()
    go_t[...] = dot(w_ref[...], cot_ref[...], 1, 1).astype(BF16)
    for h in range(HEADS):
        relay_pair(h)
    relay_near(0)
    relay_near(1)
    relay_far(0)
    last_arrivals(0)
    attend(0)
    back_first(0)
    weight_core(0)
    relay_near(2)
    relay_far(1)
    last_arrivals(1)
    attend(1)
    back_first(1)
    weight_core(1)
    relay_near(3)
    relay_far(2)
    back_far(0)
    weight_x(0)
    last_arrivals(2)
    attend(2)
    back_first(2)
    weight_core(2)
    relay_far(3)
    back_far(1)
    back_near(0)
    weight_x(1)
    last_arrivals(3)
    attend(3)
    back_first(3)
    weight_core(3)
    back_far(2)
    back_near(1)
    back_pair(0)
    weight_x(2)
    weight_x(3)
    for part in range(4):
        cols = slice(part * 512, (part + 1) * 512)
        mixed_ref[:, cols] = dot(att_t[...], w_ref[:, cols], 0, 0).astype(BF16)
    store = pltpu.make_async_copy(mixed_ref, mixed_hbm, load_sem.at[2])
    store.start()
    back_far(3)
    back_near(2)
    back_pair(1)
    weight_y()
    back_near(3)
    back_pair(2)
    weight_z()
    finish(0)
    back_pair(3)
    finish(1)
    finish(2)
    weight_end()
    finish(3)
    store.wait()
    for when, copy in started:
        if when is None:
            copy.wait_send()
        else:
            pl.when(when)(copy.wait_send)


SENDS = 112


def shards(queries, keys, values, out_weight, cotangent, prefix):
    vmem = pl.BlockSpec(memory_space=pltpu.VMEM)
    anywhere = pl.BlockSpec(memory_space=pl.ANY)
    pair = (HEADS, 2)
    mixed, dq, dk, dv, dw = pl.pallas_call(
        kernel,
        out_shape=(
            jax.ShapeDtypeStruct((TOK, D), BF16),
            jax.ShapeDtypeStruct((TOK, HD), F32),
            jax.ShapeDtypeStruct((TOK, HD), F32),
            jax.ShapeDtypeStruct((TOK, HD), F32),
            jax.ShapeDtypeStruct((2, D), F32),
        ),
        in_specs=[pl.BlockSpec(memory_space=pltpu.SMEM), vmem, vmem, vmem, anywhere, anywhere],
        out_specs=(anywhere, vmem, vmem, vmem, vmem),
        scratch_shapes=[
            pltpu.VMEM((HD, D), BF16),
            pltpu.VMEM((TOK, D), BF16),
            pltpu.VMEM((TOK, D), BF16),
            pltpu.VMEM(pair + (KEYS, HEAD_DIM), BF16),
            pltpu.VMEM(pair + (128, HEAD_DIM), BF16),
            pltpu.VMEM(pair + (64, HEAD_DIM), BF16),
            pltpu.VMEM(pair + (128, HEAD_DIM), BF16),
            pltpu.VMEM((KEYS, TOK), F32),
            pltpu.VMEM((HD, TOK), BF16),
            pltpu.VMEM((HD, TOK), BF16),
            pltpu.VMEM(pair + (3 * BLOCK, HEAD_DIM), F32),
            pltpu.VMEM(pair + (8 * BLOCK, HEAD_DIM), BF16),
            pltpu.VMEM((HEADS, 10, 2, BLOCK, HEAD_DIM), BF16),
            pltpu.VMEM((HEADS, 64, D), BF16),
            pltpu.VMEM((HEADS, 64, D), BF16),
            pltpu.VMEM((HEADS, 64, D), BF16),
            pltpu.VMEM((3, 64, D), BF16),
            pltpu.VMEM((64, D), F32),
            pltpu.VMEM((64, D), BF16),
            pltpu.VMEM((3, 16, D), BF16),
            pltpu.VMEM((8, 2, D), F32),
            pltpu.VMEM((7, 2, D), F32),
            pltpu.SemaphoreType.DMA((3,)),
            pltpu.SemaphoreType.DMA((SENDS,)),
            pltpu.SemaphoreType.DMA((HEADS, KINDS)),
            pltpu.SemaphoreType.DMA((13,)),
        ],
        compiler_params=pltpu.CompilerParams(
            collective_id=0, has_side_effects=True, vmem_limit_bytes=56 << 20
        ),
        cost_estimate=pl.CostEstimate(
            flops=3_700_000_000, bytes_accessed=8_000_000, transcendentals=1_400_000
        ),
        name="hier_attention",
    )(prefix, queries[0], keys[0], values[0], out_weight, cotangent[0])
    return mixed[None], dq[None], dk[None], dv[None], dw


def solution(mesh):
    tokens = P("dp", "ctx", None)
    return jax.shard_map(
        shards,
        mesh=mesh,
        in_specs=(tokens, tokens, tokens, P(), tokens, P("dp")),
        out_specs=(tokens, tokens, tokens, tokens, P(("dp", "ctx"), None)),
        check_vma=False,
    )
```

```python
import jax
import jax.numpy as jnp
from jax import lax
from jax.experimental import pallas as pl
from jax.experimental.pallas import tpu as pltpu
from jax.sharding import PartitionSpec as P

HEADS = 4
HEAD_DIM = 128
BLOCK = 128
D = 2048
HD = 512
TOK = 256
LEN = 8192
CTX = 32
KEYS = 1280
SCALE = HEAD_DIM**-0.5
LOG2E = 1.4426950408889634
DEAD = -1e30
MESH = pl.DeviceIdType.MESH
F32 = jnp.float32
BF16 = jnp.bfloat16

PREV, OWN, NEXT, NEAR1, FAR1, THIRD1, NEAR2, FAR2, COPY2 = 0, 1, 3, 4, 5, 6, 7, 8, 9

(
    R_PREV,
    R_NEXT,
    R_NEAR1,
    R_FAR1,
    R_THIRD1,
    R_PAIR,
    R_NEAR2,
    R_FAR2,
    R_COPY2,
    B_PREV,
    B_NEXT,
    B_NEAR1,
    B_FAR1,
    B_THIRD1,
    B_COPY2,
    B_FAR2,
    B_NEAR2,
    B_PIECE,
    W_CORE,
) = range(19)
KINDS = 19
G_PREV, G_NEXT, G_NEAR1, G_FAR1, G_THIRD1, G_COPY2, G_FAR2, G_NEAR2 = range(8)


def dot(a, b, ca, cb):
    return lax.dot_general(a, b, (((ca,), (cb,)), ((), ())), preferred_element_type=F32)


def slot(index, count=1):
    return pl.ds(index * BLOCK, count * BLOCK)


def kernel(
    prefix_ref,
    q_hbm,
    k_hbm,
    v_hbm,
    w_hbm,
    cot_hbm,
    mixed_hbm,
    dq_ref,
    dk_ref,
    dv_ref,
    dw_ref,
    q_ref,
    k_ref,
    v_ref,
    w_ref,
    cot_ref,
    mixed_ref,
    win,
    co1,
    co2,
    bias,
    go_t,
    att_t,
    keep,
    gsend,
    grecv,
    piece_grad,
    rs_core_send,
    rs_core_recv,
    rs_x_send,
    rs_x_recv,
    rs_own,
    rs_y_send,
    rs_y_recv,
    rs_z_send,
    rs_z_recv,
    load_sem,
    send_sem,
    recv_sem,
    rs_recv_sem,
):
    dp = lax.axis_index("dp")
    me = lax.axis_index("ctx")
    x, core = lax.div(dp, 2), lax.rem(dp, 2)
    y, z = lax.div(me, 8), lax.rem(me, 8)
    r = lax.rem(me, 4)
    parity = lax.rem(me, 2)
    pi = 1 - 2 * parity
    tau = 1 - 2 * lax.div(r, 2)
    outer = (r == 0) | (r == 3)
    inner = (r == 1) | (r == 2)

    def ctx(offset):
        return (dp, lax.rem(me + offset + 2 * CTX, CTX))

    def row_peer(step):
        return (dp, y * 8 + lax.rem(z + step, 8))

    def column_peer(step):
        return (dp, lax.rem(y + step, 4) * 8 + z)

    sibling = (dp + 1 - 2 * core, me)

    barrier = pltpu.get_barrier_semaphore()
    partners = [ctx(o) for o in (1, -1, 2, -2, 6, -6, 7, -7, 8, -8, 16)]
    partners += [row_peer(s) for s in range(1, 8)]
    partners += [(lax.rem(x + s, 4) * 2 + core, me) for s in range(1, 4)]
    partners += [sibling]
    for partner in partners:
        pl.semaphore_signal(barrier, inc=1, device_id=partner, device_id_type=MESH)

    loads = [
        pltpu.make_async_copy(source, target, load_sem.at[index])
        for index, (source, target) in enumerate(
            (
                (k_hbm, k_ref),
                (v_hbm, v_ref),
                (q_hbm, q_ref),
                (w_hbm, w_ref),
                (cot_hbm, cot_ref),
            )
        )
    ]
    for load in loads:
        load.start()

    half = pl.multiple_of(parity * 64, 64)
    other_half = pl.multiple_of(64 - parity * 64, 64)
    entry = lax.broadcasted_iota(jnp.int32, (192, TOK), 0)
    token = lax.broadcasted_iota(jnp.int32, (192, TOK), 1)
    mean1 = (entry < 128) & (lax.shift_right_logical(token, 1) == entry)
    mean2 = (entry >= 128) & (lax.shift_right_logical(token, 2) == entry - 128)
    means = jnp.where(mean1, 0.5, jnp.where(mean2, 0.25, 0.0)).astype(BF16)
    for kv, source in enumerate((k_ref, v_ref)):
        loads[kv].wait()
        coarse = dot(means, source[...], 1, 0).astype(BF16)
        for h in range(HEADS):
            cols = slice(h * HEAD_DIM, (h + 1) * HEAD_DIM)
            win[h, kv, OWN * BLOCK : (OWN + 2) * BLOCK, :] = source[:, cols]
            co1[h, kv] = coarse[:128, cols]
            co2[h, kv] = coarse[128:, cols]

    pl.semaphore_wait(barrier, len(partners))

    started = []

    def send(sems, kind, src, dst, device, when=None):
        send_sems, recv_sems = sems
        copy = pltpu.make_async_remote_copy(
            src_ref=src,
            dst_ref=dst,
            send_sem=send_sems.at[len(started)],
            recv_sem=recv_sems.at[kind],
            device_id=device,
            device_id_type=MESH,
        )
        if when is None:
            copy.start()
        else:
            pl.when(when)(copy.start)
        started.append((when, copy))

    def arrive(sems, kind, dst, device):
        pltpu.make_async_remote_copy(
            src_ref=dst,
            dst_ref=dst,
            send_sem=sems[0].at[0],
            recv_sem=sems[1].at[kind],
            device_id=device,
            device_id_type=MESH,
        ).wait_recv()

    def sems(h):
        return send_sem, recv_sem.at[h]

    def window(h, index):
        return win.at[h, :, slot(index), :]

    def returned(h, index):
        return grecv.at[h, index]

    def send_level2(h):
        piece = co2.at[h]
        rows = pl.ds(pl.multiple_of(NEAR2 * BLOCK + half, 64), 64)
        send(sems(h), R_NEAR2, piece, win.at[h, :, rows, :], ctx(7 * tau), outer)
        send(sems(h), R_PAIR, piece, win.at[h, :, rows, :], ctx(6 * tau), inner)

    def send_level1(h):
        send(sems(h), R_NEAR1, co1.at[h], window(h, NEAR1), ctx(2 * pi))
        send(sems(h), R_FAR1, co1.at[h], window(h, FAR1), ctx(-2 * pi))

    def send_fine(h):
        send(sems(h), R_NEXT, window(h, OWN), window(h, NEXT), ctx(-1))
        send(sems(h), R_PREV, window(h, OWN + 1), window(h, PREV), ctx(1))

    def relay_near(h):
        @pl.when(outer)
        def _():
            first = pl.ds(pl.multiple_of(NEAR2 * BLOCK + other_half, 64), 64)
            second = pl.ds(pl.multiple_of(NEAR2 * BLOCK + half, 64), 64)
            arrive(sems(h), R_NEAR2, win.at[h, :, first, :], ctx(tau))
            arrive(sems(h), R_PAIR, win.at[h, :, second, :], ctx(tau))

        @pl.when(inner)
        def _():
            arrive(sems(h), R_NEAR2, window(h, NEAR2), ctx(tau))

        send(sems(h), R_NEAR2, window(h, NEAR2), window(h, NEAR2), ctx(tau), outer)
        send(sems(h), R_FAR2, window(h, NEAR2), window(h, FAR2), ctx(tau), inner)

    def relay_third(h):
        arrive(sems(h), R_NEAR1, window(h, NEAR1), ctx(2 * pi))
        send(sems(h), R_THIRD1, window(h, NEAR1), window(h, THIRD1), ctx(pi))

    def relay_far(h):
        arrive(sems(h), R_FAR2, window(h, FAR2), ctx(tau))
        send(sems(h), R_FAR2, window(h, FAR2), window(h, FAR2), ctx(-tau), inner)
        send(sems(h), R_COPY2, window(h, FAR2), window(h, COPY2), ctx(-8 * tau))

    def last_arrivals(h):
        arrive(sems(h), R_NEXT, window(h, NEXT), ctx(1))
        arrive(sems(h), R_PREV, window(h, PREV), ctx(-1))
        arrive(sems(h), R_FAR1, window(h, FAR1), ctx(2 * pi))
        arrive(sems(h), R_THIRD1, window(h, THIRD1), ctx(pi))
        arrive(sems(h), R_COPY2, window(h, COPY2), ctx(8 * tau))

    def masks():
        prefix_end = prefix_ref[0] * BLOCK
        first_row = me * TOK
        key = lax.broadcasted_iota(jnp.int32, (4 * BLOCK, TOK), 0)
        query = lax.broadcasted_iota(jnp.int32, (4 * BLOCK, TOK), 1)
        apart = lax.shift_right_logical(key, 7) - lax.shift_right_logical(query, 7)
        column = first_row - BLOCK + key
        live = (apart >= 0) & (apart <= 2) & (column >= 0) & (column < LEN)
        live = live & ((column < prefix_end) | (column <= first_row + query))
        bias[: 4 * BLOCK, :] = jnp.where(live, 0.0, DEAD)
        quad = lax.div(me, 4)
        near2 = jnp.where(tau == 1, 2 * quad + 3, 2 * quad - 2)
        far2 = jnp.where(tau == 1, 2 * quad - 2, 2 * quad + 3)
        copy2 = jnp.where(tau == 1, 2 * quad + 2, 2 * quad - 1)
        level1 = [(NEAR1, me - 2 * pi), (FAR1, me + 2 * pi), (THIRD1, me + 3 * pi)]
        level2 = [(NEAR2, near2), (FAR2, far2), (COPY2, copy2)]
        place = lax.broadcasted_iota(jnp.int32, (BLOCK, TOK), 0)
        for level, entries in ((1, level1), (2, level2)):
            blocks = LEN // (BLOCK << level)
            own = lax.div(me, level)
            for index, block in entries:
                end = (block * BLOCK + place + 1) * (1 << level)
                inside = (block >= 0) & (block < blocks)
                before = jnp.where(inside & (block < own), LEN, 0)
                until = jnp.where(inside, prefix_end, 0)
                usable = (place < before) | ((end <= until) & (end > 0))
                bias[slot(index), :] = jnp.where(usable, float(level), DEAD)

    def attend(h):
        cols = slice(h * HEAD_DIM, (h + 1) * HEAD_DIM)
        key = win[h, 0]
        value = win[h, 1]
        query = q_ref[:, cols]
        scores = dot(key, query, 1, 1) * (SCALE * LOG2E) + bias[...]
        peak = jnp.max(scores, axis=0, keepdims=True)
        weighted = jnp.exp2(scores - peak)
        inverse = 1.0 / jnp.sum(weighted, axis=0, keepdims=True)
        weighted_half = weighted.astype(BF16)
        attended = (dot(value, weighted_half, 0, 0) * inverse).astype(BF16)
        att_t[cols, :] = attended
        back = go_t[cols, :].astype(F32)
        delta = jnp.sum(back * attended.astype(F32), axis=0, keepdims=True) * inverse
        back = (back * inverse).astype(BF16)
        score_grad = (weighted * (dot(value, back, 1, 0) - delta)).astype(BF16)
        dq_ref[:, cols] = jnp.transpose(dot(key, score_grad, 0, 0) * SCALE)
        for kv, grad in enumerate(
            (dot(score_grad, query, 1, 0) * SCALE, dot(weighted_half, back, 1, 1))
        ):
            own = dk_ref if kv == 0 else dv_ref
            own[:, cols] = grad[OWN * BLOCK : (OWN + 2) * BLOCK]
            gsend[h, kv, slot(0), :] = grad[:BLOCK].astype(BF16)
            gsend[h, kv, slot(1), :] = grad[NEXT * BLOCK : (NEXT + 1) * BLOCK].astype(BF16)
            gsend[h, kv, slot(2), :] = grad[FAR1 * BLOCK : (FAR1 + 1) * BLOCK].astype(BF16)
            gsend[h, kv, slot(3), :] = grad[THIRD1 * BLOCK : (THIRD1 + 1) * BLOCK].astype(BF16)
            gsend[h, kv, slot(4), :] = grad[COPY2 * BLOCK :].astype(BF16)
            keep[h, kv, slot(0), :] = grad[NEAR1 * BLOCK : (NEAR1 + 1) * BLOCK]
            keep[h, kv, slot(1), :] = grad[FAR2 * BLOCK : (FAR2 + 1) * BLOCK]
            keep[h, kv, slot(2), :] = grad[NEAR2 * BLOCK : (NEAR2 + 1) * BLOCK]

    def outgoing(h, index):
        return gsend.at[h, :, slot(index), :]

    def back_copy(h):
        send(sems(h), B_COPY2, outgoing(h, 4), returned(h, G_COPY2), ctx(8 * tau))

    def back_pass(h):
        send(sems(h), B_THIRD1, outgoing(h, 3), returned(h, G_THIRD1), ctx(pi))

    def back_level1(h):
        send(sems(h), B_FAR1, outgoing(h, 2), returned(h, G_FAR1), ctx(2 * pi))

    def back_fine(h):
        send(sems(h), B_NEXT, outgoing(h, 0), returned(h, G_NEXT), ctx(-1))
        send(sems(h), B_PREV, outgoing(h, 1), returned(h, G_PREV), ctx(1))

    def back_far(h):
        arrive(sems(h), B_COPY2, returned(h, G_COPY2), ctx(-8 * tau))
        own = keep[h, :, slot(1), :] + grecv[h, G_COPY2].astype(F32)
        keep[h, :, slot(1), :] = own

        @pl.when(inner)
        def _():
            arrive(sems(h), B_FAR2, returned(h, G_FAR2), ctx(-tau))
            keep[h, :, slot(1), :] = own + grecv[h, G_FAR2].astype(F32)

        gsend[h, :, slot(6), :] = keep[h, :, slot(1), :].astype(BF16)
        send(sems(h), B_FAR2, outgoing(h, 6), returned(h, G_FAR2), ctx(tau), outer)
        send(sems(h), B_NEAR2, outgoing(h, 6), returned(h, G_NEAR2), ctx(tau), inner)

    def back_third(h):
        arrive(sems(h), B_THIRD1, returned(h, G_THIRD1), ctx(pi))
        theirs = grecv[h, G_THIRD1].astype(F32)
        gsend[h, :, slot(5), :] = (keep[h, :, slot(0), :] + theirs).astype(BF16)
        send(sems(h), B_NEAR1, outgoing(h, 5), returned(h, G_NEAR1), ctx(-2 * pi))

    def back_near(h):
        arrive(sems(h), B_NEAR2, returned(h, G_NEAR2), ctx(tau))
        theirs = grecv[h, G_NEAR2].astype(F32)
        gsend[h, :, slot(7), :] = (keep[h, :, slot(2), :] + theirs).astype(BF16)
        send(sems(h), B_NEAR2, outgoing(h, 7), returned(h, G_NEAR2), ctx(-tau), inner)
        first = pl.ds(pl.multiple_of(7 * BLOCK + other_half, 64), 64)
        second = pl.ds(pl.multiple_of(7 * BLOCK + half, 64), 64)
        send(sems(h), B_PIECE, gsend.at[h, :, first, :], piece_grad.at[h], ctx(7 * tau), outer)
        send(sems(h), B_PIECE, gsend.at[h, :, second, :], piece_grad.at[h], ctx(6 * tau), outer)

    def finish(h):
        cols = slice(h * HEAD_DIM, (h + 1) * HEAD_DIM)
        arrive(sems(h), B_NEXT, returned(h, G_NEXT), ctx(1))
        arrive(sems(h), B_PREV, returned(h, G_PREV), ctx(-1))
        arrive(sems(h), B_FAR1, returned(h, G_FAR1), ctx(-2 * pi))
        arrive(sems(h), B_NEAR1, returned(h, G_NEAR1), ctx(2 * pi))
        arrive(sems(h), B_PIECE, piece_grad.at[h], ctx(7 * tau))
        for kv, own in enumerate((dk_ref, dv_ref)):
            level1 = grecv[h, G_FAR1, kv].astype(F32) + grecv[h, G_NEAR1, kv].astype(F32)
            entries = jnp.concatenate([level1.astype(BF16), piece_grad[h, kv]], axis=0)
            spread = dot(means, entries, 0, 0)
            own[:BLOCK, cols] += spread[:BLOCK] + grecv[h, G_PREV, kv].astype(F32)
            own[BLOCK:, cols] += spread[BLOCK:] + grecv[h, G_NEXT, kv].astype(F32)

    def weight_part(h, which):
        rows = pl.ds(pl.multiple_of(h * HEAD_DIM + which * 64, 64), 64)
        return dot(att_t[rows, :], cot_ref[...], 1, 0)

    def weight_core(h):
        rs_core_send[h] = weight_part(h, 1 - core).astype(BF16)
        send(sems(h), W_CORE, rs_core_send.at[h], rs_core_recv.at[h], sibling)

    rs_sems = (send_sem, rs_recv_sem)

    def weight_x(h):
        arrive(sems(h), W_CORE, rs_core_recv.at[h], sibling)
        total = weight_part(h, core) + rs_core_recv[h].astype(F32)
        rs_x_send[h] = total.astype(BF16)

        @pl.when(x == h)
        def _():
            rs_own[...] = total

        step = lax.rem(x - h + 4, 4)
        place = jnp.maximum(step - 1, 0)
        send(rs_sems, place, rs_x_send.at[h], rs_x_recv.at[place], (h * 2 + core, me), x != h)

    def weight_y():
        for step in range(1, 4):
            device = (lax.rem(x + step, 4) * 2 + core, me)
            arrive(rs_sems, step - 1, rs_x_recv.at[step - 1], device)
        total = rs_own[...]
        for step in range(1, 4):
            total = total + rs_x_recv[step - 1].astype(F32)
        rs_own[...] = total
        rs_y_send[...] = total.astype(BF16)
        for step in range(1, 4):
            rows = pl.ds(pl.multiple_of(lax.rem(y + step, 4) * 16, 16), 16)
            send(rs_sems, 2 + step, rs_y_send.at[rows], rs_y_recv.at[step - 1], column_peer(step))

    def weight_z():
        for step in range(1, 4):
            arrive(rs_sems, 2 + step, rs_y_recv.at[step - 1], column_peer(step))
        total = rs_own[pl.ds(pl.multiple_of(y * 16, 16), 16), :]
        for step in range(1, 4):
            total = total + rs_y_recv[step - 1].astype(F32)
        for part in range(8):
            rs_z_send[part] = total[2 * part : 2 * part + 2]
        for step in range(1, 8):
            part = rs_z_send.at[lax.rem(z + step, 8)]
            send(rs_sems, 5 + step, part, rs_z_recv.at[step - 1], row_peer(step))

    def weight_end():
        for step in range(1, 8):
            arrive(rs_sems, 5 + step, rs_z_recv.at[step - 1], row_peer(step))
        total = rs_z_send[z]
        for step in range(1, 8):
            total = total + rs_z_recv[step - 1]
        dw_ref[...] = total

    send_level2(0)
    send_level2(1)
    send_level2(2)
    send_level2(3)
    send_level1(0)
    send_level1(1)
    send_level1(2)
    send_level1(3)
    send_fine(0)
    send_fine(1)
    send_fine(2)
    send_fine(3)
    masks()
    for load in loads[2:]:
        load.wait()
    go_t[...] = dot(w_ref[...], cot_ref[...], 1, 1).astype(BF16)
    relay_near(0)
    relay_near(1)
    relay_near(2)
    relay_near(3)
    relay_far(0)
    relay_far(1)
    relay_far(2)
    relay_far(3)
    relay_third(0)
    relay_third(1)
    relay_third(2)
    relay_third(3)
    last_arrivals(0)
    attend(0)
    back_copy(0)
    back_pass(0)
    back_level1(0)
    last_arrivals(1)
    attend(1)
    back_copy(1)
    back_pass(1)
    back_level1(1)
    back_far(0)
    last_arrivals(2)
    attend(2)
    back_copy(2)
    back_pass(2)
    back_level1(2)
    back_far(1)
    last_arrivals(3)
    attend(3)
    back_copy(3)
    back_pass(3)
    back_level1(3)
    back_far(2)
    back_near(0)
    weight_core(0)
    weight_core(1)
    weight_core(2)
    weight_core(3)
    back_far(3)
    back_near(1)
    back_fine(0)
    weight_x(0)
    weight_x(1)
    weight_x(2)
    weight_x(3)
    back_near(2)
    back_fine(1)
    back_fine(2)
    back_fine(3)
    back_third(0)
    back_third(1)
    back_third(2)
    back_third(3)
    back_near(3)
    for part in range(4):
        cols = slice(part * 512, (part + 1) * 512)
        mixed_ref[:, cols] = dot(att_t[...], w_ref[:, cols], 0, 0).astype(BF16)
    store = pltpu.make_async_copy(mixed_ref, mixed_hbm, load_sem.at[5])
    store.start()
    weight_y()
    weight_z()
    finish(0)
    finish(1)
    finish(2)
    weight_end()
    finish(3)
    store.wait()
    for when, copy in started:
        if when is None:
            copy.wait_send()
        else:
            pl.when(when)(copy.wait_send)


SENDS = 112


def hand_over(*refs):
    sources, targets, buffers, in_sems, out_sems = refs[:5], refs[5:10], refs[10:15], refs[15], refs[16]
    stages = []
    for i in range(5):
        rows = sources[i].shape[0]
        parts = 1 if i == 4 else 4 if i == 0 else 2
        for part in range(parts):
            size = rows // parts
            span = pl.ds(part * size, size)
            n = len(stages)
            stages.append(
                (
                    pltpu.make_async_copy(sources[i].at[span], buffers[i].at[span], in_sems.at[n]),
                    pltpu.make_async_copy(buffers[i].at[span], targets[i].at[span], out_sems.at[n]),
                )
            )
    for fetch, _ in stages:
        fetch.start()
    for fetch, store in stages:
        fetch.wait()
        store.start()
    for _, store in stages:
        store.wait()


def shards(queries, keys, values, out_weight, cotangent, prefix):
    vmem = pl.BlockSpec(memory_space=pltpu.VMEM)
    anywhere = pl.BlockSpec(memory_space=pl.ANY)
    pair = (HEADS, 2)
    mixed, dq, dk, dv, dw = pl.pallas_call(
        kernel,
        out_shape=(
            jax.ShapeDtypeStruct((TOK, D), BF16),
            jax.ShapeDtypeStruct((TOK, HD), F32),
            jax.ShapeDtypeStruct((TOK, HD), F32),
            jax.ShapeDtypeStruct((TOK, HD), F32),
            jax.ShapeDtypeStruct((2, D), F32),
        ),
        in_specs=[pl.BlockSpec(memory_space=pltpu.SMEM)] + [anywhere] * 5,
        out_specs=(anywhere, vmem, vmem, vmem, vmem),
        scratch_shapes=[
            pltpu.VMEM((TOK, HD), BF16),
            pltpu.VMEM((TOK, HD), BF16),
            pltpu.VMEM((TOK, HD), BF16),
            pltpu.VMEM((HD, D), BF16),
            pltpu.VMEM((TOK, D), BF16),
            pltpu.VMEM((TOK, D), BF16),
            pltpu.VMEM(pair + (KEYS, HEAD_DIM), BF16),
            pltpu.VMEM(pair + (128, HEAD_DIM), BF16),
            pltpu.VMEM(pair + (64, HEAD_DIM), BF16),
            pltpu.VMEM((KEYS, TOK), F32),
            pltpu.VMEM((HD, TOK), BF16),
            pltpu.VMEM((HD, TOK), BF16),
            pltpu.VMEM(pair + (3 * BLOCK, HEAD_DIM), F32),
            pltpu.VMEM(pair + (8 * BLOCK, HEAD_DIM), BF16),
            pltpu.VMEM((HEADS, 8, 2, BLOCK, HEAD_DIM), BF16),
            pltpu.VMEM(pair + (64, HEAD_DIM), BF16),
            pltpu.VMEM((HEADS, 64, D), BF16),
            pltpu.VMEM((HEADS, 64, D), BF16),
            pltpu.VMEM((HEADS, 64, D), BF16),
            pltpu.VMEM((3, 64, D), BF16),
            pltpu.VMEM((64, D), F32),
            pltpu.VMEM((64, D), BF16),
            pltpu.VMEM((3, 16, D), BF16),
            pltpu.VMEM((8, 2, D), F32),
            pltpu.VMEM((7, 2, D), F32),
            pltpu.SemaphoreType.DMA((6,)),
            pltpu.SemaphoreType.DMA((SENDS,)),
            pltpu.SemaphoreType.DMA((HEADS, KINDS)),
            pltpu.SemaphoreType.DMA((13,)),
        ],
        compiler_params=pltpu.CompilerParams(
            collective_id=0, has_side_effects=True, vmem_limit_bytes=56 << 20
        ),
        cost_estimate=pl.CostEstimate(
            flops=3_700_000_000, bytes_accessed=8_000_000, transcendentals=1_400_000
        ),
        name="hier_attention",
    )(prefix, queries[0], keys[0], values[0], out_weight, cotangent[0])
    results = (mixed, dq, dk, dv, dw)
    mixed, dq, dk, dv, dw = pl.pallas_call(
        hand_over,
        out_shape=tuple(jax.ShapeDtypeStruct(a.shape, a.dtype) for a in results),
        in_specs=[anywhere] * 5,
        out_specs=(anywhere,) * 5,
        scratch_shapes=[pltpu.VMEM(a.shape, a.dtype) for a in results]
        + [pltpu.SemaphoreType.DMA((11,)), pltpu.SemaphoreType.DMA((11,))],
        name="hand_over",
    )(*results)
    return mixed[None], dq[None], dk[None], dv[None], dw


def solution(mesh):
    tokens = P("dp", "ctx", None)
    return jax.shard_map(
        shards,
        mesh=mesh,
        in_specs=(tokens, tokens, tokens, P(), tokens, P("dp")),
        out_specs=(tokens, tokens, tokens, tokens, P(("dp", "ctx"), None)),
        check_vma=False,
    )
```

```python
import jax
import jax.numpy as jnp
from jax import lax
from jax.experimental import pallas as pl
from jax.experimental.pallas import tpu as pltpu
from jax.sharding import PartitionSpec as P

HEADS = 4
HEAD_DIM = 128
BLOCK = 128
D = 2048
HD = 512
TOK = 256
LEN = 8192
CTX = 32
KEYS = 1280
WIDE = D // 2
SCALE = HEAD_DIM**-0.5
LOG2E = 1.4426950408889634
DEAD = -1e30
MESH = pl.DeviceIdType.MESH
F32 = jnp.float32
BF16 = jnp.bfloat16

PREV, OWN, NEXT, NEAR1, FAR1, THIRD1, NEAR2, FAR2, COPY2 = 0, 1, 3, 4, 5, 6, 7, 8, 9

(
    R_PREV,
    R_NEXT,
    R_NEAR1,
    R_FAR1,
    R_THIRD1,
    R_PAIR,
    R_NEAR2,
    R_FAR2,
    R_COPY2,
    B_PREV,
    B_NEXT,
    B_NEAR1,
    B_FAR1,
    B_THIRD1,
    B_COPY2,
    B_FAR2,
    B_NEAR2,
    B_PIECE,
    W_CORE,
) = range(19)
KINDS = 19
G_PREV, G_NEXT, G_NEAR1, G_FAR1, G_THIRD1, G_COPY2, G_FAR2, G_NEAR2 = range(8)


def dot(a, b, ca, cb):
    return lax.dot_general(a, b, (((ca,), (cb,)), ((), ())), preferred_element_type=F32)


def slot(index, count=1):
    return pl.ds(index * BLOCK, count * BLOCK)


def kernel(
    prefix_ref,
    q_hbm,
    k_hbm,
    v_hbm,
    w_hbm,
    cot_hbm,
    mixed_hbm,
    dq_ref,
    dk_ref,
    dv_ref,
    dw_ref,
    q_ref,
    k_ref,
    v_ref,
    w_ref,
    cot_ref,
    mixed_ref,
    win,
    co1,
    co2,
    bias,
    go_t,
    att_t,
    keep,
    gsend,
    grecv,
    piece_grad,
    rs_part,
    rs_core_send,
    rs_core_recv,
    rs_left,
    rs_right,
    rs_left_x,
    rs_left_own,
    rs_left_send,
    rs_left_y,
    rs_right_y,
    rs_right_own,
    rs_right_send,
    rs_right_x,
    rs_z_send,
    rs_z_recv,
    load_sem,
    send_sem,
    recv_sem,
    rs_recv_sem,
):
    dp = lax.axis_index("dp")
    me = lax.axis_index("ctx")
    x, core = lax.div(dp, 2), lax.rem(dp, 2)
    y, z = lax.div(me, 8), lax.rem(me, 8)
    r = lax.rem(me, 4)
    parity = lax.rem(me, 2)
    pi = 1 - 2 * parity
    tau = 1 - 2 * lax.div(r, 2)
    outer = (r == 0) | (r == 3)
    inner = (r == 1) | (r == 2)

    def ctx(offset):
        return (dp, lax.rem(me + offset + 2 * CTX, CTX))

    def row_peer(step):
        return (dp, y * 8 + lax.rem(z + step, 8))

    def column_peer(step):
        return (dp, lax.rem(y + step, 4) * 8 + z)

    sibling = (dp + 1 - 2 * core, me)

    barrier = pltpu.get_barrier_semaphore()
    partners = [ctx(o) for o in (1, -1, 2, -2, 6, -6, 7, -7, 8, -8, 16)]
    partners += [row_peer(s) for s in range(1, 8)]
    partners += [(lax.rem(x + s, 4) * 2 + core, me) for s in range(1, 4)]
    partners += [sibling]
    for partner in partners:
        pl.semaphore_signal(barrier, inc=1, device_id=partner, device_id_type=MESH)

    loads = [
        pltpu.make_async_copy(source, target, load_sem.at[index])
        for index, (source, target) in enumerate(
            (
                (k_hbm, k_ref),
                (v_hbm, v_ref),
                (q_hbm, q_ref),
                (w_hbm, w_ref),
                (cot_hbm, cot_ref),
            )
        )
    ]
    for load in loads:
        load.start()

    half = pl.multiple_of(parity * 64, 64)
    other_half = pl.multiple_of(64 - parity * 64, 64)
    entry = lax.broadcasted_iota(jnp.int32, (192, TOK), 0)
    token = lax.broadcasted_iota(jnp.int32, (192, TOK), 1)
    mean1 = (entry < 128) & (lax.shift_right_logical(token, 1) == entry)
    mean2 = (entry >= 128) & (lax.shift_right_logical(token, 2) == entry - 128)
    means = jnp.where(mean1, 0.5, jnp.where(mean2, 0.25, 0.0)).astype(BF16)
    for kv, source in enumerate((k_ref, v_ref)):
        loads[kv].wait()
        coarse = dot(means, source[...], 1, 0).astype(BF16)
        for h in range(HEADS):
            cols = slice(h * HEAD_DIM, (h + 1) * HEAD_DIM)
            win[h, kv, OWN * BLOCK : (OWN + 2) * BLOCK, :] = source[:, cols]
            co1[h, kv] = coarse[:128, cols]
            co2[h, kv] = coarse[128:, cols]

    pl.semaphore_wait(barrier, len(partners))

    started = []

    def send(sems, kind, src, dst, device, when=None):
        send_sems, recv_sems = sems
        copy = pltpu.make_async_remote_copy(
            src_ref=src,
            dst_ref=dst,
            send_sem=send_sems.at[len(started)],
            recv_sem=recv_sems.at[kind],
            device_id=device,
            device_id_type=MESH,
        )
        if when is None:
            copy.start()
        else:
            pl.when(when)(copy.start)
        started.append((when, copy))

    def arrive(sems, kind, dst, device):
        pltpu.make_async_remote_copy(
            src_ref=dst,
            dst_ref=dst,
            send_sem=sems[0].at[0],
            recv_sem=sems[1].at[kind],
            device_id=device,
            device_id_type=MESH,
        ).wait_recv()

    def sems(h):
        return send_sem, recv_sem.at[h]

    def window(h, index):
        return win.at[h, :, slot(index), :]

    def returned(h, index):
        return grecv.at[h, index]

    def send_level2(h):
        piece = co2.at[h]
        rows = pl.ds(pl.multiple_of(NEAR2 * BLOCK + half, 64), 64)
        send(sems(h), R_NEAR2, piece, win.at[h, :, rows, :], ctx(7 * tau), outer)
        send(sems(h), R_PAIR, piece, win.at[h, :, rows, :], ctx(6 * tau), inner)

    def send_level1(h):
        send(sems(h), R_NEAR1, co1.at[h], window(h, NEAR1), ctx(2 * pi))
        send(sems(h), R_FAR1, co1.at[h], window(h, FAR1), ctx(-2 * pi))

    def send_fine(h):
        send(sems(h), R_NEXT, window(h, OWN), window(h, NEXT), ctx(-1))
        send(sems(h), R_PREV, window(h, OWN + 1), window(h, PREV), ctx(1))

    def relay_near(h):
        @pl.when(outer)
        def _():
            first = pl.ds(pl.multiple_of(NEAR2 * BLOCK + other_half, 64), 64)
            second = pl.ds(pl.multiple_of(NEAR2 * BLOCK + half, 64), 64)
            arrive(sems(h), R_NEAR2, win.at[h, :, first, :], ctx(tau))
            arrive(sems(h), R_PAIR, win.at[h, :, second, :], ctx(tau))

        @pl.when(inner)
        def _():
            arrive(sems(h), R_NEAR2, window(h, NEAR2), ctx(tau))

        send(sems(h), R_NEAR2, window(h, NEAR2), window(h, NEAR2), ctx(tau), outer)
        send(sems(h), R_FAR2, window(h, NEAR2), window(h, FAR2), ctx(tau), inner)

    def relay_third(h):
        arrive(sems(h), R_NEAR1, window(h, NEAR1), ctx(2 * pi))
        send(sems(h), R_THIRD1, window(h, NEAR1), window(h, THIRD1), ctx(pi))

    def relay_far(h):
        arrive(sems(h), R_FAR2, window(h, FAR2), ctx(tau))
        send(sems(h), R_FAR2, window(h, FAR2), window(h, FAR2), ctx(-tau), inner)
        send(sems(h), R_COPY2, window(h, FAR2), window(h, COPY2), ctx(-8 * tau))

    def last_arrivals(h):
        arrive(sems(h), R_NEXT, window(h, NEXT), ctx(1))
        arrive(sems(h), R_PREV, window(h, PREV), ctx(-1))
        arrive(sems(h), R_FAR1, window(h, FAR1), ctx(2 * pi))
        arrive(sems(h), R_THIRD1, window(h, THIRD1), ctx(pi))
        arrive(sems(h), R_COPY2, window(h, COPY2), ctx(8 * tau))

    def masks():
        prefix_end = prefix_ref[0] * BLOCK
        first_row = me * TOK
        key = lax.broadcasted_iota(jnp.int32, (4 * BLOCK, TOK), 0)
        query = lax.broadcasted_iota(jnp.int32, (4 * BLOCK, TOK), 1)
        apart = lax.shift_right_logical(key, 7) - lax.shift_right_logical(query, 7)
        column = first_row - BLOCK + key
        live = (apart >= 0) & (apart <= 2) & (column >= 0) & (column < LEN)
        live = live & ((column < prefix_end) | (column <= first_row + query))
        bias[: 4 * BLOCK, :] = jnp.where(live, 0.0, DEAD)
        quad = lax.div(me, 4)
        near2 = jnp.where(tau == 1, 2 * quad + 3, 2 * quad - 2)
        far2 = jnp.where(tau == 1, 2 * quad - 2, 2 * quad + 3)
        copy2 = jnp.where(tau == 1, 2 * quad + 2, 2 * quad - 1)
        level1 = [(NEAR1, me - 2 * pi), (FAR1, me + 2 * pi), (THIRD1, me + 3 * pi)]
        level2 = [(NEAR2, near2), (FAR2, far2), (COPY2, copy2)]
        place = lax.broadcasted_iota(jnp.int32, (BLOCK, TOK), 0)
        for level, entries in ((1, level1), (2, level2)):
            blocks = LEN // (BLOCK << level)
            own = lax.div(me, level)
            for index, block in entries:
                end = (block * BLOCK + place + 1) * (1 << level)
                inside = (block >= 0) & (block < blocks)
                before = jnp.where(inside & (block < own), LEN, 0)
                until = jnp.where(inside, prefix_end, 0)
                usable = (place < before) | ((end <= until) & (end > 0))
                bias[slot(index), :] = jnp.where(usable, float(level), DEAD)

    def attend(h):
        cols = slice(h * HEAD_DIM, (h + 1) * HEAD_DIM)
        key = win[h, 0]
        value = win[h, 1]
        query = q_ref[:, cols]
        scores = dot(key, query, 1, 1) * (SCALE * LOG2E) + bias[...]
        peak = jnp.max(scores, axis=0, keepdims=True)
        weighted = jnp.exp2(scores - peak)
        inverse = 1.0 / jnp.sum(weighted, axis=0, keepdims=True)
        weighted_half = weighted.astype(BF16)
        attended = (dot(value, weighted_half, 0, 0) * inverse).astype(BF16)
        att_t[cols, :] = attended
        back = go_t[cols, :].astype(F32)
        delta = jnp.sum(back * attended.astype(F32), axis=0, keepdims=True) * inverse
        back = (back * inverse).astype(BF16)
        score_grad = (weighted * (dot(value, back, 1, 0) - delta)).astype(BF16)
        dq_ref[:, cols] = jnp.transpose(dot(key, score_grad, 0, 0) * SCALE)
        for kv, grad in enumerate(
            (dot(score_grad, query, 1, 0) * SCALE, dot(weighted_half, back, 1, 1))
        ):
            own = dk_ref if kv == 0 else dv_ref
            own[:, cols] = grad[OWN * BLOCK : (OWN + 2) * BLOCK]
            gsend[h, kv, slot(0), :] = grad[:BLOCK].astype(BF16)
            gsend[h, kv, slot(1), :] = grad[NEXT * BLOCK : (NEXT + 1) * BLOCK].astype(BF16)
            gsend[h, kv, slot(2), :] = grad[FAR1 * BLOCK : (FAR1 + 1) * BLOCK].astype(BF16)
            gsend[h, kv, slot(3), :] = grad[THIRD1 * BLOCK : (THIRD1 + 1) * BLOCK].astype(BF16)
            gsend[h, kv, slot(4), :] = grad[COPY2 * BLOCK :].astype(BF16)
            keep[h, kv, slot(0), :] = grad[NEAR1 * BLOCK : (NEAR1 + 1) * BLOCK]
            keep[h, kv, slot(1), :] = grad[FAR2 * BLOCK : (FAR2 + 1) * BLOCK]
            keep[h, kv, slot(2), :] = grad[NEAR2 * BLOCK : (NEAR2 + 1) * BLOCK]

    def outgoing(h, index):
        return gsend.at[h, :, slot(index), :]

    def back_copy(h):
        send(sems(h), B_COPY2, outgoing(h, 4), returned(h, G_COPY2), ctx(8 * tau))

    def back_pass(h):
        send(sems(h), B_THIRD1, outgoing(h, 3), returned(h, G_THIRD1), ctx(pi))

    def back_level1(h):
        send(sems(h), B_FAR1, outgoing(h, 2), returned(h, G_FAR1), ctx(2 * pi))

    def back_fine(h):
        send(sems(h), B_NEXT, outgoing(h, 0), returned(h, G_NEXT), ctx(-1))
        send(sems(h), B_PREV, outgoing(h, 1), returned(h, G_PREV), ctx(1))

    def back_far(h):
        arrive(sems(h), B_COPY2, returned(h, G_COPY2), ctx(-8 * tau))
        own = keep[h, :, slot(1), :] + grecv[h, G_COPY2].astype(F32)
        keep[h, :, slot(1), :] = own

        @pl.when(inner)
        def _():
            arrive(sems(h), B_FAR2, returned(h, G_FAR2), ctx(-tau))
            keep[h, :, slot(1), :] = own + grecv[h, G_FAR2].astype(F32)

        gsend[h, :, slot(6), :] = keep[h, :, slot(1), :].astype(BF16)
        send(sems(h), B_FAR2, outgoing(h, 6), returned(h, G_FAR2), ctx(tau), outer)
        send(sems(h), B_NEAR2, outgoing(h, 6), returned(h, G_NEAR2), ctx(tau), inner)

    def back_third(h):
        arrive(sems(h), B_THIRD1, returned(h, G_THIRD1), ctx(pi))
        theirs = grecv[h, G_THIRD1].astype(F32)
        gsend[h, :, slot(5), :] = (keep[h, :, slot(0), :] + theirs).astype(BF16)
        send(sems(h), B_NEAR1, outgoing(h, 5), returned(h, G_NEAR1), ctx(-2 * pi))

    def back_near(h):
        arrive(sems(h), B_NEAR2, returned(h, G_NEAR2), ctx(tau))
        theirs = grecv[h, G_NEAR2].astype(F32)
        gsend[h, :, slot(7), :] = (keep[h, :, slot(2), :] + theirs).astype(BF16)
        send(sems(h), B_NEAR2, outgoing(h, 7), returned(h, G_NEAR2), ctx(-tau), inner)
        first = pl.ds(pl.multiple_of(7 * BLOCK + other_half, 64), 64)
        second = pl.ds(pl.multiple_of(7 * BLOCK + half, 64), 64)
        send(sems(h), B_PIECE, gsend.at[h, :, first, :], piece_grad.at[h], ctx(7 * tau), outer)
        send(sems(h), B_PIECE, gsend.at[h, :, second, :], piece_grad.at[h], ctx(6 * tau), outer)

    def finish(h):
        cols = slice(h * HEAD_DIM, (h + 1) * HEAD_DIM)
        arrive(sems(h), B_NEXT, returned(h, G_NEXT), ctx(1))
        arrive(sems(h), B_PREV, returned(h, G_PREV), ctx(-1))
        arrive(sems(h), B_FAR1, returned(h, G_FAR1), ctx(-2 * pi))
        arrive(sems(h), B_NEAR1, returned(h, G_NEAR1), ctx(2 * pi))
        arrive(sems(h), B_PIECE, piece_grad.at[h], ctx(7 * tau))
        for kv, own in enumerate((dk_ref, dv_ref)):
            level1 = grecv[h, G_FAR1, kv].astype(F32) + grecv[h, G_NEAR1, kv].astype(F32)
            entries = jnp.concatenate([level1.astype(BF16), piece_grad[h, kv]], axis=0)
            spread = dot(means, entries, 0, 0)
            own[:BLOCK, cols] += spread[:BLOCK] + grecv[h, G_PREV, kv].astype(F32)
            own[BLOCK:, cols] += spread[BLOCK:] + grecv[h, G_NEXT, kv].astype(F32)

    def weight_core(h):
        theirs = pl.ds(pl.multiple_of(h * HEAD_DIM + (1 - core) * 64, 64), 64)
        ours = pl.ds(pl.multiple_of(h * HEAD_DIM + core * 64, 64), 64)
        rows = jnp.concatenate([att_t[theirs, :], att_t[ours, :]], axis=0)
        part = dot(rows, cot_ref[...], 1, 0)
        rs_core_send[h] = part[:64].astype(BF16)
        rs_part[h] = part[64:]
        send(sems(h), W_CORE, rs_core_send.at[h], rs_core_recv.at[h], sibling)

    rs_sems = (send_sem, rs_recv_sem)

    def weight_first(h):
        arrive(sems(h), W_CORE, rs_core_recv.at[h], sibling)
        total = rs_part[h] + rs_core_recv[h].astype(F32)
        rs_part[h] = total
        rs_left[h] = total[:, :WIDE].astype(BF16)
        rs_right[h] = total[:, WIDE:].astype(BF16)
        place = jnp.maximum(lax.rem(x - h + 4, 4) - 1, 0)
        device = (h * 2 + core, me)
        send(rs_sems, place, rs_left.at[h], rs_left_x.at[place], device, x != h)
        if h % 2 == 1:
            for step in range(1, 4):
                rows = pl.ds(pl.multiple_of(lax.rem(y + step, 4) * 16, 16), 16)
                pair = pl.ds(h - 1, 2)
                source = rs_right.at[pair, rows, :]
                target = rs_right_y.at[step - 1, pair]
                send(rs_sems, 3 * (h // 2) + 2 + step, source, target, column_peer(step))

    def weight_left():
        for step in range(1, 4):
            device = (lax.rem(x + step, 4) * 2 + core, me)
            arrive(rs_sems, step - 1, rs_left_x.at[step - 1], device)
        total = rs_part[x, :, :WIDE]
        for step in range(1, 4):
            total = total + rs_left_x[step - 1].astype(F32)
        rs_left_own[...] = total
        rs_left_send[...] = total.astype(BF16)
        for step in range(1, 4):
            rows = pl.ds(pl.multiple_of(lax.rem(y + step, 4) * 16, 16), 16)
            source = rs_left_send.at[rows]
            send(rs_sems, 10 + step, source, rs_left_y.at[step - 1], column_peer(step))

    def weight_right():
        for h in (1, 3):
            for step in range(1, 4):
                part = rs_right_y.at[step - 1, pl.ds(h - 1, 2)]
                arrive(rs_sems, 3 * (h // 2) + 2 + step, part, column_peer(step))
        total = rs_part[:, pl.ds(pl.multiple_of(y * 16, 16), 16), WIDE:]
        for step in range(1, 4):
            total = total + rs_right_y[step - 1].astype(F32)
        rs_right_own[...] = total
        rs_right_send[...] = total.astype(BF16)
        for step in range(1, 4):
            head = lax.rem(x + step, 4)
            device = (head * 2 + core, me)
            send(rs_sems, 13 + step, rs_right_send.at[head], rs_right_x.at[step - 1], device)

    def weight_z():
        left = rs_left_own[pl.ds(pl.multiple_of(y * 16, 16), 16), :]
        right = rs_right_own[x]
        for step in range(1, 4):
            arrive(rs_sems, 10 + step, rs_left_y.at[step - 1], column_peer(step))
            device = (lax.rem(x + step, 4) * 2 + core, me)
            arrive(rs_sems, 13 + step, rs_right_x.at[step - 1], device)
        for step in range(1, 4):
            left = left + rs_left_y[step - 1].astype(F32)
            right = right + rs_right_x[step - 1].astype(F32)
        for part in range(8):
            rs_z_send[part, :, :WIDE] = left[2 * part : 2 * part + 2]
            rs_z_send[part, :, WIDE:] = right[2 * part : 2 * part + 2]
        for step in range(1, 8):
            part = rs_z_send.at[lax.rem(z + step, 8)]
            send(rs_sems, 16 + step, part, rs_z_recv.at[step - 1], row_peer(step))

    def weight_end():
        for step in range(1, 8):
            arrive(rs_sems, 16 + step, rs_z_recv.at[step - 1], row_peer(step))
        total = rs_z_send[z]
        for step in range(1, 8):
            total = total + rs_z_recv[step - 1]
        dw_ref[...] = total

    send_level2(0)
    send_level2(1)
    send_level2(2)
    send_level2(3)
    send_level1(0)
    send_level1(1)
    send_level1(2)
    send_fine(0)
    send_fine(1)
    send_fine(2)
    send_level1(3)
    masks()
    for load in loads[2:]:
        load.wait()
    go_t[...] = dot(w_ref[...], cot_ref[...], 1, 1).astype(BF16)
    relay_near(0)
    relay_near(1)
    relay_near(2)
    relay_near(3)
    relay_far(0)
    relay_far(1)
    relay_far(2)
    send_fine(3)
    relay_third(0)
    relay_third(1)
    relay_third(2)
    last_arrivals(0)
    attend(0)
    back_copy(0)
    back_pass(0)
    last_arrivals(1)
    attend(1)
    back_copy(1)
    back_pass(1)
    relay_far(3)
    relay_third(3)
    back_level1(0)
    back_far(0)
    last_arrivals(2)
    attend(2)
    back_copy(2)
    back_pass(2)
    back_level1(1)
    back_far(1)
    last_arrivals(3)
    attend(3)
    back_copy(3)
    back_pass(3)
    back_level1(2)
    weight_core(0)
    weight_core(1)
    weight_core(2)
    weight_core(3)
    back_level1(3)
    back_far(2)
    back_near(0)
    back_far(3)
    weight_first(0)
    weight_first(1)
    weight_first(2)
    weight_first(3)
    back_near(1)
    back_fine(0)
    back_near(2)
    back_fine(1)
    back_fine(2)
    back_fine(3)
    back_third(0)
    back_third(1)
    back_third(2)
    back_third(3)
    weight_left()
    weight_right()
    back_near(3)
    weight_z()
    for part in range(4):
        cols = slice(part * 512, (part + 1) * 512)
        mixed_ref[:, cols] = dot(att_t[...], w_ref[:, cols], 0, 0).astype(BF16)
    store = pltpu.make_async_copy(mixed_ref, mixed_hbm, load_sem.at[5])
    store.start()
    finish(0)
    finish(1)
    finish(2)
    weight_end()
    finish(3)
    store.wait()
    for when, copy in started:
        if when is None:
            copy.wait_send()
        else:
            pl.when(when)(copy.wait_send)


SENDS = 128


def hand_over(*refs):
    sources, targets, buffers, in_sems, out_sems = refs[:5], refs[5:10], refs[10:15], refs[15], refs[16]
    stages = []
    for i in range(5):
        rows = sources[i].shape[0]
        parts = 1 if i == 4 else 4 if i == 0 else 2
        for part in range(parts):
            size = rows // parts
            span = pl.ds(part * size, size)
            n = len(stages)
            stages.append(
                (
                    pltpu.make_async_copy(sources[i].at[span], buffers[i].at[span], in_sems.at[n]),
                    pltpu.make_async_copy(buffers[i].at[span], targets[i].at[span], out_sems.at[n]),
                )
            )
    for fetch, _ in stages:
        fetch.start()
    for fetch, store in stages:
        fetch.wait()
        store.start()
    for _, store in stages:
        store.wait()


def shards(queries, keys, values, out_weight, cotangent, prefix):
    vmem = pl.BlockSpec(memory_space=pltpu.VMEM)
    anywhere = pl.BlockSpec(memory_space=pl.ANY)
    pair = (HEADS, 2)
    mixed, dq, dk, dv, dw = pl.pallas_call(
        kernel,
        out_shape=(
            jax.ShapeDtypeStruct((TOK, D), BF16),
            jax.ShapeDtypeStruct((TOK, HD), F32),
            jax.ShapeDtypeStruct((TOK, HD), F32),
            jax.ShapeDtypeStruct((TOK, HD), F32),
            jax.ShapeDtypeStruct((2, D), F32),
        ),
        in_specs=[pl.BlockSpec(memory_space=pltpu.SMEM)] + [anywhere] * 5,
        out_specs=(anywhere, vmem, vmem, vmem, vmem),
        scratch_shapes=[
            pltpu.VMEM((TOK, HD), BF16),
            pltpu.VMEM((TOK, HD), BF16),
            pltpu.VMEM((TOK, HD), BF16),
            pltpu.VMEM((HD, D), BF16),
            pltpu.VMEM((TOK, D), BF16),
            pltpu.VMEM((TOK, D), BF16),
            pltpu.VMEM(pair + (KEYS, HEAD_DIM), BF16),
            pltpu.VMEM(pair + (128, HEAD_DIM), BF16),
            pltpu.VMEM(pair + (64, HEAD_DIM), BF16),
            pltpu.VMEM((KEYS, TOK), F32),
            pltpu.VMEM((HD, TOK), BF16),
            pltpu.VMEM((HD, TOK), BF16),
            pltpu.VMEM(pair + (3 * BLOCK, HEAD_DIM), F32),
            pltpu.VMEM(pair + (8 * BLOCK, HEAD_DIM), BF16),
            pltpu.VMEM((HEADS, 8, 2, BLOCK, HEAD_DIM), BF16),
            pltpu.VMEM(pair + (64, HEAD_DIM), BF16),
            pltpu.VMEM((HEADS, 64, D), F32),
            pltpu.VMEM((HEADS, 64, D), BF16),
            pltpu.VMEM((HEADS, 64, D), BF16),
            pltpu.VMEM((HEADS, 64, WIDE), BF16),
            pltpu.VMEM((HEADS, 64, WIDE), BF16),
            pltpu.VMEM((3, 64, WIDE), BF16),
            pltpu.VMEM((64, WIDE), F32),
            pltpu.VMEM((64, WIDE), BF16),
            pltpu.VMEM((3, 16, WIDE), BF16),
            pltpu.VMEM((3, HEADS, 16, WIDE), BF16),
            pltpu.VMEM((HEADS, 16, WIDE), F32),
            pltpu.VMEM((HEADS, 16, WIDE), BF16),
            pltpu.VMEM((3, 16, WIDE), BF16),
            pltpu.VMEM((8, 2, D), F32),
            pltpu.VMEM((7, 2, D), F32),
            pltpu.SemaphoreType.DMA((6,)),
            pltpu.SemaphoreType.DMA((SENDS,)),
            pltpu.SemaphoreType.DMA((HEADS, KINDS)),
            pltpu.SemaphoreType.DMA((24,)),
        ],
        compiler_params=pltpu.CompilerParams(
            collective_id=0, has_side_effects=True, vmem_limit_bytes=56 << 20
        ),
        cost_estimate=pl.CostEstimate(
            flops=3_700_000_000, bytes_accessed=8_000_000, transcendentals=1_400_000
        ),
        name="hier_attention",
    )(prefix, queries[0], keys[0], values[0], out_weight, cotangent[0])
    results = (mixed, dq, dk, dv, dw)
    mixed, dq, dk, dv, dw = pl.pallas_call(
        hand_over,
        out_shape=tuple(jax.ShapeDtypeStruct(a.shape, a.dtype) for a in results),
        in_specs=[anywhere] * 5,
        out_specs=(anywhere,) * 5,
        scratch_shapes=[pltpu.VMEM(a.shape, a.dtype) for a in results]
        + [pltpu.SemaphoreType.DMA((11,)), pltpu.SemaphoreType.DMA((11,))],
        name="hand_over",
    )(*results)
    return mixed[None], dq[None], dk[None], dv[None], dw


def solution(mesh):
    tokens = P("dp", "ctx", None)
    return jax.shard_map(
        shards,
        mesh=mesh,
        in_specs=(tokens, tokens, tokens, P(), tokens, P("dp")),
        out_specs=(tokens, tokens, tokens, tokens, P(("dp", "ctx"), None)),
        check_vma=False,
    )
```

```python
import jax
import jax.numpy as jnp
from jax import lax
from jax.experimental import pallas as pl
from jax.experimental.pallas import tpu as pltpu
from jax.sharding import PartitionSpec as P

HEADS = 4
HEAD_DIM = 128
BLOCK = 128
D = 2048
HD = 512
TOK = 256
LEN = 8192
CTX = 32
KEYS = 1280
WIDE = D // 2
SCALE = HEAD_DIM**-0.5
LOG2E = 1.4426950408889634
DEAD = -1e30
MESH = pl.DeviceIdType.MESH
F32 = jnp.float32
BF16 = jnp.bfloat16

PREV, OWN, NEXT, NEAR1, FAR1, THIRD1, NEAR2, FAR2, COPY2 = 0, 1, 3, 4, 5, 6, 7, 8, 9

(
    R_PREV,
    R_NEXT,
    R_NEAR1,
    R_FAR1,
    R_THIRD1,
    R_PAIR,
    R_NEAR2,
    R_FAR2,
    R_COPY2,
    B_PREV,
    B_NEXT,
    B_NEAR1,
    B_FAR1,
    B_THIRD1,
    B_COPY2,
    B_FAR2,
    B_NEAR2,
    B_PIECE,
    W_CORE,
) = range(19)
KINDS = 19
G_PREV, G_NEXT, G_NEAR1, G_FAR1, G_THIRD1, G_COPY2, G_FAR2, G_NEAR2 = range(8)


def dot(a, b, ca, cb):
    return lax.dot_general(a, b, (((ca,), (cb,)), ((), ())), preferred_element_type=F32)


def slot(index, count=1):
    return pl.ds(index * BLOCK, count * BLOCK)


def kernel(
    prefix_ref,
    q_hbm,
    k_hbm,
    v_hbm,
    w_hbm,
    cot_hbm,
    mixed_hbm,
    dq_ref,
    dk_ref,
    dv_ref,
    dw_ref,
    q_ref,
    k_ref,
    v_ref,
    w_ref,
    cot_ref,
    mixed_ref,
    win,
    co1,
    co2,
    bias,
    go_t,
    att_t,
    keep,
    gsend,
    grecv,
    piece_grad,
    rs_part,
    rs_core_send,
    rs_core_recv,
    rs_left,
    rs_right,
    rs_left_x,
    rs_left_own,
    rs_left_send,
    rs_left_y,
    rs_right_y,
    rs_right_own,
    rs_right_send,
    rs_right_x,
    rs_z_send,
    rs_z_recv,
    load_sem,
    send_sem,
    recv_sem,
    rs_recv_sem,
):
    dp = lax.axis_index("dp")
    me = lax.axis_index("ctx")
    x, core = lax.div(dp, 2), lax.rem(dp, 2)
    y, z = lax.div(me, 8), lax.rem(me, 8)
    r = lax.rem(me, 4)
    parity = lax.rem(me, 2)
    pi = 1 - 2 * parity
    tau = 1 - 2 * lax.div(r, 2)
    outer = (r == 0) | (r == 3)
    inner = (r == 1) | (r == 2)

    def ctx(offset):
        return (dp, lax.rem(me + offset + 2 * CTX, CTX))

    def row_peer(step):
        return (dp, y * 8 + lax.rem(z + step, 8))

    def column_peer(step):
        return (dp, lax.rem(y + step, 4) * 8 + z)

    sibling = (dp + 1 - 2 * core, me)

    loads = [
        pltpu.make_async_copy(source, target, load_sem.at[index])
        for index, (source, target) in enumerate(
            (
                (k_hbm, k_ref),
                (v_hbm, v_ref),
                (q_hbm, q_ref),
                (w_hbm, w_ref),
                (cot_hbm, cot_ref),
            )
        )
    ]
    for load in loads:
        load.start()

    barrier = pltpu.get_barrier_semaphore()
    partners = [ctx(o) for o in (1, -1, 2, -2, 6, -6, 7, -7, 8, -8, 16)]
    partners += [row_peer(s) for s in range(1, 8)]
    partners += [(lax.rem(x + s, 4) * 2 + core, me) for s in range(1, 4)]
    partners += [sibling]
    for partner in partners:
        pl.semaphore_signal(barrier, inc=1, device_id=partner, device_id_type=MESH)

    def masks():
        prefix_end = prefix_ref[0] * BLOCK
        first_row = me * TOK
        key = lax.broadcasted_iota(jnp.int32, (4 * BLOCK, TOK), 0)
        query = lax.broadcasted_iota(jnp.int32, (4 * BLOCK, TOK), 1)
        apart = lax.shift_right_logical(key, 7) - lax.shift_right_logical(query, 7)
        column = first_row - BLOCK + key
        live = (apart >= 0) & (apart <= 2) & (column >= 0) & (column < LEN)
        live = live & ((column < prefix_end) | (column <= first_row + query))
        bias[: 4 * BLOCK, :] = jnp.where(live, 0.0, DEAD)
        quad = lax.div(me, 4)
        near2 = jnp.where(tau == 1, 2 * quad + 3, 2 * quad - 2)
        far2 = jnp.where(tau == 1, 2 * quad - 2, 2 * quad + 3)
        copy2 = jnp.where(tau == 1, 2 * quad + 2, 2 * quad - 1)
        level1 = [(NEAR1, me - 2 * pi), (FAR1, me + 2 * pi), (THIRD1, me + 3 * pi)]
        level2 = [(NEAR2, near2), (FAR2, far2), (COPY2, copy2)]
        place = lax.broadcasted_iota(jnp.int32, (BLOCK, TOK), 0)
        for level, entries in ((1, level1), (2, level2)):
            blocks = LEN // (BLOCK << level)
            own = lax.div(me, level)
            for index, block in entries:
                end = (block * BLOCK + place + 1) * (1 << level)
                inside = (block >= 0) & (block < blocks)
                before = jnp.where(inside & (block < own), LEN, 0)
                until = jnp.where(inside, prefix_end, 0)
                usable = (place < before) | ((end <= until) & (end > 0))
                bias[slot(index), :] = jnp.where(usable, float(level), DEAD)

    masks()

    half = pl.multiple_of(parity * 64, 64)
    other_half = pl.multiple_of(64 - parity * 64, 64)
    entry = lax.broadcasted_iota(jnp.int32, (192, TOK), 0)
    token = lax.broadcasted_iota(jnp.int32, (192, TOK), 1)
    mean1 = (entry < 128) & (lax.shift_right_logical(token, 1) == entry)
    mean2 = (entry >= 128) & (lax.shift_right_logical(token, 2) == entry - 128)
    means = jnp.where(mean1, 0.5, jnp.where(mean2, 0.25, 0.0)).astype(BF16)
    for kv, source in enumerate((k_ref, v_ref)):
        loads[kv].wait()
        coarse = dot(means, source[...], 1, 0).astype(BF16)
        for h in range(HEADS):
            cols = slice(h * HEAD_DIM, (h + 1) * HEAD_DIM)
            win[h, kv, OWN * BLOCK : (OWN + 2) * BLOCK, :] = source[:, cols]
            co1[h, kv] = coarse[:128, cols]
            co2[h, kv] = coarse[128:, cols]

    pl.semaphore_wait(barrier, len(partners))

    started = []

    def send(sems, kind, src, dst, device, when=None):
        send_sems, recv_sems = sems
        copy = pltpu.make_async_remote_copy(
            src_ref=src,
            dst_ref=dst,
            send_sem=send_sems.at[len(started)],
            recv_sem=recv_sems.at[kind],
            device_id=device,
            device_id_type=MESH,
        )
        if when is None:
            copy.start()
        else:
            pl.when(when)(copy.start)
        started.append((when, copy))

    def arrive(sems, kind, dst, device):
        pltpu.make_async_remote_copy(
            src_ref=dst,
            dst_ref=dst,
            send_sem=sems[0].at[0],
            recv_sem=sems[1].at[kind],
            device_id=device,
            device_id_type=MESH,
        ).wait_recv()

    def sems(h):
        return send_sem, recv_sem.at[h]

    def window(h, index):
        return win.at[h, :, slot(index), :]

    def returned(h, index):
        return grecv.at[h, index]

    def send_level2(h):
        piece = co2.at[h]
        rows = pl.ds(pl.multiple_of(NEAR2 * BLOCK + half, 64), 64)
        send(sems(h), R_NEAR2, piece, win.at[h, :, rows, :], ctx(7 * tau), outer)
        send(sems(h), R_PAIR, piece, win.at[h, :, rows, :], ctx(6 * tau), inner)

    def send_level1(h):
        send(sems(h), R_NEAR1, co1.at[h], window(h, NEAR1), ctx(2 * pi))
        send(sems(h), R_FAR1, co1.at[h], window(h, FAR1), ctx(-2 * pi))

    def send_fine(h):
        send(sems(h), R_NEXT, window(h, OWN), window(h, NEXT), ctx(-1))
        send(sems(h), R_PREV, window(h, OWN + 1), window(h, PREV), ctx(1))

    def relay_near(h):
        @pl.when(outer)
        def _():
            first = pl.ds(pl.multiple_of(NEAR2 * BLOCK + other_half, 64), 64)
            second = pl.ds(pl.multiple_of(NEAR2 * BLOCK + half, 64), 64)
            arrive(sems(h), R_NEAR2, win.at[h, :, first, :], ctx(tau))
            arrive(sems(h), R_PAIR, win.at[h, :, second, :], ctx(tau))

        @pl.when(inner)
        def _():
            arrive(sems(h), R_NEAR2, window(h, NEAR2), ctx(tau))

        send(sems(h), R_NEAR2, window(h, NEAR2), window(h, NEAR2), ctx(tau), outer)
        send(sems(h), R_FAR2, window(h, NEAR2), window(h, FAR2), ctx(tau), inner)

    def relay_third(h):
        arrive(sems(h), R_NEAR1, window(h, NEAR1), ctx(2 * pi))
        send(sems(h), R_THIRD1, window(h, NEAR1), window(h, THIRD1), ctx(pi))

    def relay_far(h):
        arrive(sems(h), R_FAR2, window(h, FAR2), ctx(tau))
        send(sems(h), R_FAR2, window(h, FAR2), window(h, FAR2), ctx(-tau), inner)
        send(sems(h), R_COPY2, window(h, FAR2), window(h, COPY2), ctx(-8 * tau))

    def last_arrivals(h):
        arrive(sems(h), R_NEXT, window(h, NEXT), ctx(1))
        arrive(sems(h), R_PREV, window(h, PREV), ctx(-1))
        arrive(sems(h), R_FAR1, window(h, FAR1), ctx(2 * pi))
        arrive(sems(h), R_THIRD1, window(h, THIRD1), ctx(pi))
        arrive(sems(h), R_COPY2, window(h, COPY2), ctx(8 * tau))

    def attend(h):
        cols = slice(h * HEAD_DIM, (h + 1) * HEAD_DIM)
        key = win[h, 0]
        value = win[h, 1]
        query = q_ref[:, cols]
        scores = dot(key, query, 1, 1) * (SCALE * LOG2E) + bias[...]
        peak = jnp.max(scores, axis=0, keepdims=True)
        weighted = jnp.exp2(scores - peak)
        inverse = 1.0 / jnp.sum(weighted, axis=0, keepdims=True)
        weighted_half = weighted.astype(BF16)
        attended = (dot(value, weighted_half, 0, 0) * inverse).astype(BF16)
        att_t[cols, :] = attended
        back = go_t[cols, :].astype(F32)
        delta = jnp.sum(back * attended.astype(F32), axis=0, keepdims=True) * inverse
        back = (back * inverse).astype(BF16)
        score_grad = (weighted * (dot(value, back, 1, 0) - delta)).astype(BF16)
        dq_ref[:, cols] = jnp.transpose(dot(key, score_grad, 0, 0) * SCALE)
        for kv, grad in enumerate(
            (dot(score_grad, query, 1, 0) * SCALE, dot(weighted_half, back, 1, 1))
        ):
            own = dk_ref if kv == 0 else dv_ref
            own[:, cols] = grad[OWN * BLOCK : (OWN + 2) * BLOCK]
            gsend[h, kv, slot(0), :] = grad[:BLOCK].astype(BF16)
            gsend[h, kv, slot(1), :] = grad[NEXT * BLOCK : (NEXT + 1) * BLOCK].astype(BF16)
            gsend[h, kv, slot(2), :] = grad[FAR1 * BLOCK : (FAR1 + 1) * BLOCK].astype(BF16)
            gsend[h, kv, slot(3), :] = grad[THIRD1 * BLOCK : (THIRD1 + 1) * BLOCK].astype(BF16)
            gsend[h, kv, slot(4), :] = grad[COPY2 * BLOCK :].astype(BF16)
            keep[h, kv, slot(0), :] = grad[NEAR1 * BLOCK : (NEAR1 + 1) * BLOCK]
            keep[h, kv, slot(1), :] = grad[FAR2 * BLOCK : (FAR2 + 1) * BLOCK]
            keep[h, kv, slot(2), :] = grad[NEAR2 * BLOCK : (NEAR2 + 1) * BLOCK]

    def outgoing(h, index):
        return gsend.at[h, :, slot(index), :]

    def back_copy(h):
        send(sems(h), B_COPY2, outgoing(h, 4), returned(h, G_COPY2), ctx(8 * tau))

    def back_pass(h):
        send(sems(h), B_THIRD1, outgoing(h, 3), returned(h, G_THIRD1), ctx(pi))

    def back_level1(h):
        send(sems(h), B_FAR1, outgoing(h, 2), returned(h, G_FAR1), ctx(2 * pi))

    def back_fine(h):
        send(sems(h), B_NEXT, outgoing(h, 0), returned(h, G_NEXT), ctx(-1))
        send(sems(h), B_PREV, outgoing(h, 1), returned(h, G_PREV), ctx(1))

    def back_far(h):
        arrive(sems(h), B_COPY2, returned(h, G_COPY2), ctx(-8 * tau))
        own = keep[h, :, slot(1), :] + grecv[h, G_COPY2].astype(F32)
        keep[h, :, slot(1), :] = own

        @pl.when(inner)
        def _():
            arrive(sems(h), B_FAR2, returned(h, G_FAR2), ctx(-tau))
            keep[h, :, slot(1), :] = own + grecv[h, G_FAR2].astype(F32)

        gsend[h, :, slot(6), :] = keep[h, :, slot(1), :].astype(BF16)
        send(sems(h), B_FAR2, outgoing(h, 6), returned(h, G_FAR2), ctx(tau), outer)
        send(sems(h), B_NEAR2, outgoing(h, 6), returned(h, G_NEAR2), ctx(tau), inner)

    def back_third(h):
        arrive(sems(h), B_THIRD1, returned(h, G_THIRD1), ctx(pi))
        theirs = grecv[h, G_THIRD1].astype(F32)
        gsend[h, :, slot(5), :] = (keep[h, :, slot(0), :] + theirs).astype(BF16)
        send(sems(h), B_NEAR1, outgoing(h, 5), returned(h, G_NEAR1), ctx(-2 * pi))

    def back_near(h):
        arrive(sems(h), B_NEAR2, returned(h, G_NEAR2), ctx(tau))
        theirs = grecv[h, G_NEAR2].astype(F32)
        gsend[h, :, slot(7), :] = (keep[h, :, slot(2), :] + theirs).astype(BF16)
        send(sems(h), B_NEAR2, outgoing(h, 7), returned(h, G_NEAR2), ctx(-tau), inner)
        first = pl.ds(pl.multiple_of(7 * BLOCK + other_half, 64), 64)
        second = pl.ds(pl.multiple_of(7 * BLOCK + half, 64), 64)
        send(sems(h), B_PIECE, gsend.at[h, :, first, :], piece_grad.at[h], ctx(7 * tau), outer)
        send(sems(h), B_PIECE, gsend.at[h, :, second, :], piece_grad.at[h], ctx(6 * tau), outer)

    def finish(h):
        cols = slice(h * HEAD_DIM, (h + 1) * HEAD_DIM)
        arrive(sems(h), B_NEXT, returned(h, G_NEXT), ctx(1))
        arrive(sems(h), B_PREV, returned(h, G_PREV), ctx(-1))
        arrive(sems(h), B_FAR1, returned(h, G_FAR1), ctx(-2 * pi))
        arrive(sems(h), B_NEAR1, returned(h, G_NEAR1), ctx(2 * pi))
        arrive(sems(h), B_PIECE, piece_grad.at[h], ctx(7 * tau))
        for kv, own in enumerate((dk_ref, dv_ref)):
            level1 = grecv[h, G_FAR1, kv].astype(F32) + grecv[h, G_NEAR1, kv].astype(F32)
            entries = jnp.concatenate([level1.astype(BF16), piece_grad[h, kv]], axis=0)
            spread = dot(means, entries, 0, 0)
            own[:BLOCK, cols] += spread[:BLOCK] + grecv[h, G_PREV, kv].astype(F32)
            own[BLOCK:, cols] += spread[BLOCK:] + grecv[h, G_NEXT, kv].astype(F32)

    def weight_core(h):
        theirs = pl.ds(pl.multiple_of(h * HEAD_DIM + (1 - core) * 64, 64), 64)
        ours = pl.ds(pl.multiple_of(h * HEAD_DIM + core * 64, 64), 64)
        rows = jnp.concatenate([att_t[theirs, :], att_t[ours, :]], axis=0)
        part = dot(rows, cot_ref[...], 1, 0)
        rs_core_send[h] = part[:64].astype(BF16)
        rs_part[h] = part[64:]
        send(sems(h), W_CORE, rs_core_send.at[h], rs_core_recv.at[h], sibling)

    rs_sems = (send_sem, rs_recv_sem)

    def weight_first(h):
        arrive(sems(h), W_CORE, rs_core_recv.at[h], sibling)
        total = rs_part[h] + rs_core_recv[h].astype(F32)
        rs_part[h] = total
        rs_left[h] = total[:, :WIDE].astype(BF16)
        rs_right[h] = total[:, WIDE:].astype(BF16)
        place = jnp.maximum(lax.rem(x - h + 4, 4) - 1, 0)
        device = (h * 2 + core, me)
        send(rs_sems, place, rs_left.at[h], rs_left_x.at[place], device, x != h)
        if h % 2 == 1:
            for step in range(1, 4):
                rows = pl.ds(pl.multiple_of(lax.rem(y + step, 4) * 16, 16), 16)
                pair = pl.ds(h - 1, 2)
                source = rs_right.at[pair, rows, :]
                target = rs_right_y.at[step - 1, pair]
                send(rs_sems, 3 * (h // 2) + 2 + step, source, target, column_peer(step))

    def weight_left():
        for step in range(1, 4):
            device = (lax.rem(x + step, 4) * 2 + core, me)
            arrive(rs_sems, step - 1, rs_left_x.at[step - 1], device)
        total = rs_part[x, :, :WIDE]
        for step in range(1, 4):
            total = total + rs_left_x[step - 1].astype(F32)
        rs_left_own[...] = total
        rs_left_send[...] = total.astype(BF16)
        for step in range(1, 4):
            rows = pl.ds(pl.multiple_of(lax.rem(y + step, 4) * 16, 16), 16)
            source = rs_left_send.at[rows]
            send(rs_sems, 10 + step, source, rs_left_y.at[step - 1], column_peer(step))

    def weight_right():
        for h in (1, 3):
            for step in range(1, 4):
                part = rs_right_y.at[step - 1, pl.ds(h - 1, 2)]
                arrive(rs_sems, 3 * (h // 2) + 2 + step, part, column_peer(step))
        total = rs_part[:, pl.ds(pl.multiple_of(y * 16, 16), 16), WIDE:]
        for step in range(1, 4):
            total = total + rs_right_y[step - 1].astype(F32)
        rs_right_own[...] = total
        rs_right_send[...] = total.astype(BF16)
        for step in range(1, 4):
            head = lax.rem(x + step, 4)
            device = (head * 2 + core, me)
            send(rs_sems, 13 + step, rs_right_send.at[head], rs_right_x.at[step - 1], device)

    def weight_z():
        left = rs_left_own[pl.ds(pl.multiple_of(y * 16, 16), 16), :]
        right = rs_right_own[x]
        for step in range(1, 4):
            arrive(rs_sems, 10 + step, rs_left_y.at[step - 1], column_peer(step))
            device = (lax.rem(x + step, 4) * 2 + core, me)
            arrive(rs_sems, 13 + step, rs_right_x.at[step - 1], device)
        for step in range(1, 4):
            left = left + rs_left_y[step - 1].astype(F32)
            right = right + rs_right_x[step - 1].astype(F32)
        for part in range(8):
            rs_z_send[part, :, :WIDE] = left[2 * part : 2 * part + 2]
            rs_z_send[part, :, WIDE:] = right[2 * part : 2 * part + 2]
        for step in range(1, 8):
            part = rs_z_send.at[lax.rem(z + step, 8)]
            send(rs_sems, 16 + step, part, rs_z_recv.at[step - 1], row_peer(step))

    def weight_end():
        for step in range(1, 8):
            arrive(rs_sems, 16 + step, rs_z_recv.at[step - 1], row_peer(step))
        total = rs_z_send[z]
        for step in range(1, 8):
            total = total + rs_z_recv[step - 1]
        dw_ref[...] = total

    send_level2(0)
    send_level2(1)
    send_level2(2)
    send_level2(3)
    send_level1(0)
    send_level1(1)
    send_level1(2)
    send_fine(0)
    send_fine(1)
    send_fine(2)
    send_level1(3)
    for load in loads[2:]:
        load.wait()
    go_t[...] = dot(w_ref[...], cot_ref[...], 1, 1).astype(BF16)
    relay_near(0)
    relay_near(1)
    relay_near(2)
    relay_near(3)
    relay_far(0)
    relay_far(1)
    relay_far(2)
    send_fine(3)
    relay_third(0)
    relay_third(1)
    relay_third(2)
    last_arrivals(0)
    attend(0)
    back_copy(0)
    back_pass(0)
    last_arrivals(1)
    attend(1)
    back_copy(1)
    back_pass(1)
    relay_far(3)
    relay_third(3)
    back_level1(0)
    back_far(0)
    last_arrivals(2)
    attend(2)
    back_copy(2)
    back_pass(2)
    back_level1(1)
    back_far(1)
    last_arrivals(3)
    attend(3)
    back_copy(3)
    back_pass(3)
    back_level1(2)
    weight_core(0)
    weight_core(1)
    weight_core(2)
    weight_core(3)
    back_level1(3)
    back_far(2)
    back_near(0)
    back_far(3)
    weight_first(0)
    weight_first(1)
    weight_first(2)
    weight_first(3)
    back_near(1)
    back_fine(0)
    back_near(2)
    back_fine(1)
    back_fine(2)
    back_fine(3)
    back_third(0)
    back_third(1)
    back_third(2)
    back_third(3)
    weight_left()
    weight_right()
    back_near(3)
    weight_z()
    finish(0)
    finish(1)
    finish(2)
    finish(3)
    for part in range(4):
        cols = slice(part * 512, (part + 1) * 512)
        mixed_ref[:, cols] = dot(att_t[...], w_ref[:, cols], 0, 0).astype(BF16)
    store = pltpu.make_async_copy(mixed_ref, mixed_hbm, load_sem.at[5])
    store.start()
    weight_end()
    store.wait()
    for when, copy in started:
        if when is None:
            copy.wait_send()
        else:
            pl.when(when)(copy.wait_send)


SENDS = 128


def hand_over(*refs):
    sources, targets, buffers, in_sems, out_sems = refs[:5], refs[5:10], refs[10:15], refs[15], refs[16]
    stages = []
    for i in range(5):
        rows = sources[i].shape[0]
        parts = 1 if i == 4 else 4 if i == 0 else 2
        for part in range(parts):
            size = rows // parts
            span = pl.ds(part * size, size)
            n = len(stages)
            stages.append(
                (
                    pltpu.make_async_copy(sources[i].at[span], buffers[i].at[span], in_sems.at[n]),
                    pltpu.make_async_copy(buffers[i].at[span], targets[i].at[span], out_sems.at[n]),
                )
            )
    for fetch, _ in stages:
        fetch.start()
    for fetch, store in stages:
        fetch.wait()
        store.start()
    for _, store in stages:
        store.wait()


def shards(queries, keys, values, out_weight, cotangent, prefix):
    vmem = pl.BlockSpec(memory_space=pltpu.VMEM)
    anywhere = pl.BlockSpec(memory_space=pl.ANY)
    pair = (HEADS, 2)
    mixed, dq, dk, dv, dw = pl.pallas_call(
        kernel,
        out_shape=(
            jax.ShapeDtypeStruct((TOK, D), BF16),
            jax.ShapeDtypeStruct((TOK, HD), F32),
            jax.ShapeDtypeStruct((TOK, HD), F32),
            jax.ShapeDtypeStruct((TOK, HD), F32),
            jax.ShapeDtypeStruct((2, D), F32),
        ),
        in_specs=[pl.BlockSpec(memory_space=pltpu.SMEM)] + [anywhere] * 5,
        out_specs=(anywhere, vmem, vmem, vmem, vmem),
        scratch_shapes=[
            pltpu.VMEM((TOK, HD), BF16),
            pltpu.VMEM((TOK, HD), BF16),
            pltpu.VMEM((TOK, HD), BF16),
            pltpu.VMEM((HD, D), BF16),
            pltpu.VMEM((TOK, D), BF16),
            pltpu.VMEM((TOK, D), BF16),
            pltpu.VMEM(pair + (KEYS, HEAD_DIM), BF16),
            pltpu.VMEM(pair + (128, HEAD_DIM), BF16),
            pltpu.VMEM(pair + (64, HEAD_DIM), BF16),
            pltpu.VMEM((KEYS, TOK), F32),
            pltpu.VMEM((HD, TOK), BF16),
            pltpu.VMEM((HD, TOK), BF16),
            pltpu.VMEM(pair + (3 * BLOCK, HEAD_DIM), F32),
            pltpu.VMEM(pair + (8 * BLOCK, HEAD_DIM), BF16),
            pltpu.VMEM((HEADS, 8, 2, BLOCK, HEAD_DIM), BF16),
            pltpu.VMEM(pair + (64, HEAD_DIM), BF16),
            pltpu.VMEM((HEADS, 64, D), F32),
            pltpu.VMEM((HEADS, 64, D), BF16),
            pltpu.VMEM((HEADS, 64, D), BF16),
            pltpu.VMEM((HEADS, 64, WIDE), BF16),
            pltpu.VMEM((HEADS, 64, WIDE), BF16),
            pltpu.VMEM((3, 64, WIDE), BF16),
            pltpu.VMEM((64, WIDE), F32),
            pltpu.VMEM((64, WIDE), BF16),
            pltpu.VMEM((3, 16, WIDE), BF16),
            pltpu.VMEM((3, HEADS, 16, WIDE), BF16),
            pltpu.VMEM((HEADS, 16, WIDE), F32),
            pltpu.VMEM((HEADS, 16, WIDE), BF16),
            pltpu.VMEM((3, 16, WIDE), BF16),
            pltpu.VMEM((8, 2, D), F32),
            pltpu.VMEM((7, 2, D), F32),
            pltpu.SemaphoreType.DMA((6,)),
            pltpu.SemaphoreType.DMA((SENDS,)),
            pltpu.SemaphoreType.DMA((HEADS, KINDS)),
            pltpu.SemaphoreType.DMA((24,)),
        ],
        compiler_params=pltpu.CompilerParams(
            collective_id=0, has_side_effects=True, vmem_limit_bytes=56 << 20
        ),
        cost_estimate=pl.CostEstimate(
            flops=3_700_000_000, bytes_accessed=8_000_000, transcendentals=1_400_000
        ),
        name="hier_attention",
    )(prefix, queries[0], keys[0], values[0], out_weight, cotangent[0])
    results = (mixed, dq, dk, dv, dw)
    mixed, dq, dk, dv, dw = pl.pallas_call(
        hand_over,
        out_shape=tuple(jax.ShapeDtypeStruct(a.shape, a.dtype) for a in results),
        in_specs=[anywhere] * 5,
        out_specs=(anywhere,) * 5,
        scratch_shapes=[pltpu.VMEM(a.shape, a.dtype) for a in results]
        + [pltpu.SemaphoreType.DMA((11,)), pltpu.SemaphoreType.DMA((11,))],
        name="hand_over",
    )(*results)
    return mixed[None], dq[None], dk[None], dv[None], dw


def solution(mesh):
    tokens = P("dp", "ctx", None)
    return jax.shard_map(
        shards,
        mesh=mesh,
        in_specs=(tokens, tokens, tokens, P(), tokens, P("dp")),
        out_specs=(tokens, tokens, tokens, tokens, P(("dp", "ctx"), None)),
        check_vma=False,
    )
```
